32 devices in a mesh: seq: 16 (over z, y, core), tp: 2 (over x).
Axes of the slice: x: 2, y: 2, z: 4, core: 2. Of those that a mesh axis runs over, the one named last changes fastest.
Arguments:
- residual_in: bfloat16 [4096, 1024], P('seq', 'tp'), may hold values from -6 to 6
- queries: bfloat16 [4096, 1024], P('seq', 'tp'), may hold values from -240 to 240
- keys: bfloat16 [4096, 1024], P('seq', 'tp'), may hold values from -12 to 12
- values: bfloat16 [4096, 1024], P('seq', 'tp'), may hold values from -6 to 6
- head_offset: int32 [6, 16], P(None, 'tp'), may hold values from 0 to 31
- out_weight: bfloat16 [1024, 1024], P('tp'), may hold values from -0.1875 to 0.1875
- norm_gain: float32 [1024], replicated, may hold values from 0.5 to 1.5
- gate_weight: bfloat16 [1024, 2048], P(None, 'tp'), may hold values from -0.1875 to 0.1875
- up_weight: bfloat16 [1024, 2048], P(None, 'tp'), may hold values from -0.1875 to 0.1875
- down_weight: bfloat16 [2048, 1024], P('tp'), may hold values from -0.125 to 0.125
Outputs:
- layer_out: bfloat16 [4096, 1024], P('seq', 'tp')
The draws below stay inside these ranges and needn't reach their ends.
All inputs are finite; a program needn't handle non-finite values.
Results may differ from the reference program's by a relative error of at most 0.0095.
Values may be sent and summed in bfloat16 or wider, within the bound.
No kernel may reach another device: no remote copies, remote signals or barrier semaphores. Data moves between devices by JAX's collectives and lax.ppermute only.
A program may use at most 128 MiB of HBM per device.

```python
import math
import jax
import jax.numpy as jnp
from jax import lax

D = 1024
HEADS = 16
HEAD_DIM = 64
FF = 2048
BRANCHES = 6
TOK_DEV = 256
TOKENS = 4096
WIDEST = 4096


def shared_keys(key):
    return jnp.clip(jax.random.normal(key, (TOKENS, D), jnp.float32), -6.0, 6.0)


def draw_keys(key, part):
    base = shared_keys(key)
    return base.astype(jnp.bfloat16)


def draw_queries(key, part):
    key = jax.random.fold_in(key, 5)
    return jnp.clip(2.0 * jax.random.normal(key, (TOKENS, D), jnp.float32), -12.0, 12.0).astype(jnp.bfloat16)


def place_ends(values, rng, low, top_value):
    shape = values.shape
    spot = [jax.random.randint(jax.random.fold_in(rng, axis), (), 0, shape[axis]) for axis in range(len(shape))]
    values = values.at[tuple(spot)].set(low)
    longest = shape.index(max(shape))
    spot[longest] = (spot[longest] + 1) % shape[longest]
    return values.at[tuple(spot)].set(top_value)


def levels(stream_key, dims, shards, smallest, high):
    factor_of, own = 1.0, jax.random.fold_in(stream_key, 6)
    for axis_at, blocks in shards:
        draws = jnp.exp(jax.random.uniform(jax.random.fold_in(own, axis_at), (blocks,), jnp.float32, smallest / len(shards), high / len(shards)))
        factor_of = factor_of * jnp.repeat(draws, dims[axis_at] // blocks).reshape([-1 if axis == axis_at else 1 for axis in range(len(dims))])
    return factor_of


def gaussian(stream_key, extent, deviation, most, cuts=(), kind=jnp.bfloat16):
    values = jax.random.normal(stream_key, extent, jnp.float32) * deviation
    if len(cuts) > 0:
        values = levels(stream_key, extent, cuts, -0.22, 0.18) * values
    return jnp.clip(values, min=-most, max=most).astype(kind)


def setup_inputs(seed: int = 0) -> dict:
    seeds = jax.random.split(jax.random.key(seed), 11)
    residual_in = gaussian(seeds[0], (TOKENS, D), 1.0, 6.0, ((0, 16), (1, 2)))
    queries = draw_queries(jax.random.fold_in(seeds[10], 71), 0)
    keys = draw_keys(jax.random.fold_in(seeds[10], 71), 0)
    values = gaussian(seeds[3], (TOKENS, D), 1.0, 6.0, ((0, 16), (1, 2)))
    head_offset = place_ends(jax.random.randint(seeds[4], (BRANCHES, HEADS), 0, 2 ** (BRANCHES - 1)), jax.random.fold_in(seeds[4], 1), 0, (2 ** (BRANCHES - 1)) - 1).astype(jnp.int32)
    out_weight = gaussian(seeds[5], (D, D), D ** -0.5, 0.1875, ((0, 2),))
    norm_gain = jnp.clip(jax.random.uniform(seeds[6], (D,), jnp.float32, 0.5, 1.5), 0.5, 1.5)
    gate_weight = gaussian(seeds[7], (D, FF), D ** -0.5, 0.1875, ((1, 2),))
    up_weight = gaussian(seeds[8], (D, FF), D ** -0.5, 0.1875, ((1, 2),))
    down_weight = gaussian(seeds[9], (FF, D), FF ** -0.5, 0.125, ((0, 2),))
    return {"residual_in": residual_in, "queries": queries, "keys": keys, "values": values, "head_offset": head_offset, "out_weight": out_weight, "norm_gain": norm_gain, "gate_weight": gate_weight, "up_weight": up_weight, "down_weight": down_weight}


masked_score = -1e+30

def pick_rows(array, choose, rate):
    count = array.shape[0] // rate
    shaped = array.reshape(count, rate, array.shape[1], array.shape[2])
    return lax.optimization_barrier(jnp.sum(shaped * choose[None, :, :, None].astype(array.dtype), axis=1))

def reference(residual_in, queries, keys, values, head_offset, out_weight, norm_gain, gate_weight, up_weight, down_weight):
    query_heads = queries.reshape(TOKENS, HEADS, HEAD_DIM)
    key_heads = keys.reshape(TOKENS, HEADS, HEAD_DIM)
    value_heads = values.reshape(TOKENS, HEADS, HEAD_DIM)
    scale = 1.0 / math.sqrt(HEAD_DIM)
    peak = None
    total = None
    accum = None
    for branch in range(BRANCHES):
        rate = 2 ** branch
        length = min(TOK_DEV * 2 ** (branch + 1), WIDEST)
        segments = TOKENS // length
        inner = length // rate
        offsets = head_offset[branch] % rate
        choose = jnp.arange(rate, dtype=jnp.int32)[:, None] == offsets[None, :]
        picked_query = pick_rows(query_heads, choose, rate).reshape(segments, inner, HEADS, HEAD_DIM)
        picked_key = pick_rows(key_heads, choose, rate).reshape(segments, inner, HEADS, HEAD_DIM)
        picked_value = pick_rows(value_heads, choose, rate).reshape(segments, inner, HEADS, HEAD_DIM)
        causal = jnp.arange(inner, dtype=jnp.int32)[None, :] <= jnp.arange(inner, dtype=jnp.int32)[:, None]

        def attend(block):
            query, key_rows, value_rows = block
            scores = jnp.einsum('qhd,khd->hqk', query.astype(jnp.float32), key_rows.astype(jnp.float32)) * scale
            scores = jnp.where(causal[None], scores, masked_score)
            top = lax.optimization_barrier(jnp.max(scores, axis=2, keepdims=True))
            log_total = top + jnp.log(lax.optimization_barrier(jnp.sum(jnp.exp(scores - top), axis=2, keepdims=True)))
            weights = jnp.exp(scores - log_total).astype(jnp.bfloat16)
            output = jnp.einsum('hqk,khd->qhd', weights.astype(jnp.float32), value_rows.astype(jnp.float32))
            return (output, jnp.transpose(log_total[:, :, 0]))
        outputs, logs = lax.map(attend, (picked_query, picked_key, picked_value))
        chosen = choose.astype(jnp.float32)
        count = TOKENS // rate
        spread = (outputs.reshape(count, 1, HEADS, HEAD_DIM) * chosen[None, :, :, None]).reshape(TOKENS, HEADS, HEAD_DIM)
        spread_log = jnp.broadcast_to(logs.reshape(count, 1, HEADS), (count, rate, HEADS)).reshape(TOKENS, HEADS)
        covered = jnp.broadcast_to(choose[None], (count, rate, HEADS)).reshape(TOKENS, HEADS)
        if branch == 0:
            peak = spread_log
            total = jnp.ones((TOKENS, HEADS), jnp.float32)
            accum = spread
        else:
            new_peak = jnp.where(covered, jnp.maximum(peak, spread_log), peak)
            keep = jnp.exp(peak - new_peak)
            branch_weight = jnp.where(covered, jnp.exp(jnp.where(covered, spread_log, new_peak) - new_peak), 0.0)
            total = total * keep + branch_weight
            accum = accum * keep[..., None] + branch_weight[..., None] * spread
            peak = new_peak
    mix = (accum / total[..., None]).astype(jnp.bfloat16).reshape(TOKENS, D)
    hidden = residual_in.astype(jnp.float32) + jnp.dot(mix, out_weight, preferred_element_type=jnp.float32)
    inverse = lax.rsqrt(lax.optimization_barrier(jnp.mean(hidden * hidden, axis=1, keepdims=True)) + 1e-05)
    normed = (hidden * inverse * norm_gain[None, :]).astype(jnp.bfloat16)
    gate = jnp.dot(normed, gate_weight, preferred_element_type=jnp.float32)
    up = jnp.dot(normed, up_weight, preferred_element_type=jnp.float32)
    act = (jax.nn.silu(gate) * up).astype(jnp.bfloat16)
    return (hidden + jnp.dot(act, down_weight, preferred_element_type=jnp.float32)).astype(jnp.bfloat16)
```

```python
import functools
import math

import jax
import jax.numpy as jnp
from jax import lax
from jax.experimental import pallas as pl
from jax.experimental.pallas import tpu as pltpu
from jax.sharding import PartitionSpec as P

BRANCHES = 6
LANES = 128
NEAR = 4
GROUP = LANES // NEAR
PEAK_FLOPS = 1153.5e12
MIB = 1024 * 1024
CHUNKS = 2

masked_score = -1e30


def part_rows(rows, branches):
    first, at = 0, {}
    for branch in branches:
        at[branch] = first
        first += rows // 2**branch
    return at, first


def far_sets(seq_count, rows):
    top_bits = min(seq_count.bit_length() - 1, BRANCHES)
    sets = {}
    for branch in range(2, BRANCHES):
        sets.setdefault(2 ** min(branch + 1, top_bits) // NEAR, []).append(branch)
    return sorted(sets.items())


def set_rows(sets, rows, each):
    first, at = 0, []
    for _, branches in sets:
        at.append(first)
        first += each * sum(rows // 2**branch for branch in branches)
    return at, first


def first_set(sets, step):
    return min(number for number, (span, _) in enumerate(sets) if span > step)


def even(count):
    return -(-count // 16) * 16


def mask_select(rows, branch, offset):
    rate = 2**branch
    count = rows // rate
    row = lax.broadcasted_iota(jnp.int32, (count, rows), 0)
    col = lax.broadcasted_iota(jnp.int32, (count, rows), 1)
    return jnp.where(col == row * rate + (offset & (rate - 1)), 1.0, 0.0)


def selection(rows, branches, offset_ref, head):
    select = [mask_select(rows, branch, offset_ref[branch, head]) for branch in branches]
    return jnp.concatenate(select, axis=0).astype(jnp.bfloat16)


def far_picks(sets, rows, dim, low, offset_ref, blocks, members):
    each = LANES // dim
    far_branches = range(2, BRANCHES)
    starts, _ = part_rows(rows, far_branches)
    picked = []
    for (key, value), member in zip(blocks, members):
        for head in range(each):
            lanes = slice(head * dim, (head + 1) * dim)
            select = selection(rows, far_branches, offset_ref, member * each + head)
            pairs = jnp.concatenate([key[:, lanes], value[:, lanes]], axis=1)
            picked.append(jnp.dot(select, pairs, preferred_element_type=jnp.float32))
    outs = []
    for number in range(len(blocks)):
        parts = []
        for _, branches in sets:
            for branch in branches:
                first, last = starts[branch], starts[branch] + rows // 2**branch
                parts += [picked[number * each + head][first:last] for head in range(each)]
        outs.append(jnp.concatenate(parts, axis=0).astype(jnp.bfloat16))
    return outs


def split_kernel(sets, scale, dim, offset_ref, index_ref, source_ref, *out_refs):
    wide_refs, own_ref, core_ref, chip_ref = out_refs[:2], *out_refs[2:]
    rows = source_ref.shape[0] // 3
    low = index_ref[0] % NEAR
    all_lanes = [
        pl.ds(pl.multiple_of((low ^ side) * LANES, LANES), LANES) for side in range(NEAR)
    ]
    blocks = [
        (source_ref[rows : 2 * rows, lanes], source_ref[2 * rows :, lanes]) for lanes in all_lanes[2:]
    ]
    picks = far_picks(sets, rows, dim, low, offset_ref, blocks, [low ^ 2, low ^ 3])
    for pick, wide_ref in zip(picks, wide_refs):
        wide_ref[...] = pick
    for side, lanes in enumerate(all_lanes):
        ref, first = ((own_ref, 0), (core_ref, 0), (chip_ref, 0), (core_ref, 3 * rows))[side]
        ref[first : first + rows] = source_ref[:rows, lanes] * jnp.asarray(scale, jnp.bfloat16)
        ref[first + rows : first + 3 * rows] = source_ref[rows:, lanes]


def turn_kernel(at, index_ref, *refs):
    in_refs, chip_ref, core_ref, out_refs, relay_ref = refs[:NEAR], *refs[NEAR : NEAR + 2], refs[NEAR + 2 : -1], refs[-1]
    half = chip_ref.shape[0]
    relay_ref[:half] = chip_ref[...]
    relay_ref[half:] = core_ref[half:]
    low = index_ref[0] % NEAR
    for side in range(NEAR):
        for first, out_ref in zip(at, out_refs):
            out_ref[low ^ side] = in_refs[side][first:, :]


def attend(jobs, batch):
    dim = jobs[0][0].shape[1]
    lane = lax.broadcasted_iota(jnp.int32, (1, LANES), 1)
    keys = [pairs[:, :dim] for _, pairs, _, _ in jobs]
    values = [jnp.where(lane < dim, jnp.ones_like(pairs), pairs) for _, pairs, _, _ in jobs]
    pieces = []
    for number, (query, _, _, _) in enumerate(jobs):
        block = min(128, query.shape[0])
        pieces += [(start, number, block) for start in range(0, query.shape[0], block)]
    pieces.sort(key=lambda piece: piece[0])
    done = {}
    for at in range(0, len(pieces), batch):
        now = pieces[at : at + batch]
        scores = []
        for start, number, block in now:
            query, _, before, _ = jobs[number]
            scores.append(
                lax.dot_general(
                    query[start : start + block],
                    keys[number][: before + start + block],
                    (((1,), (1,)), ((), ())),
                    preferred_element_type=jnp.float32,
                )
            )
        masked = []
        for (start, number, block), score in zip(now, scores):
            _, _, before, columns = jobs[number]
            end = before + start + block
            if before == 0 and block == 128:
                row = lax.broadcasted_iota(jnp.int32, (block, block), 0)
                col = lax.broadcasted_iota(jnp.int32, (block, block), 1)
                last = jnp.where(col <= row, score[:, start:], masked_score)
                masked.append(jnp.concatenate([score[:, :start], last], axis=1) if start else last)
            else:
                row = lax.broadcasted_iota(jnp.int32, (block, end), 0)
                allowed = columns[:, :end] <= row + (before + start)
                masked.append(jnp.where(allowed, score, masked_score))
        tops = [jnp.max(score, axis=1, keepdims=True) for score in masked]
        weights = [jnp.exp(score - top).astype(jnp.bfloat16) for score, top in zip(masked, tops)]
        for piece, weight, top in zip(now, weights, tops):
            start, number, block = piece
            end = jobs[number][2] + start + block
            accum = jnp.dot(weight, values[number][:end], preferred_element_type=jnp.float32)
            done.setdefault(number, []).append((top, accum))
    return [
        tuple(jnp.concatenate(column, axis=0) for column in zip(*done[number]))
        for number in range(len(jobs))
    ]


def top_lanes(top, count, branch):
    length = top.shape[0]
    high = top.astype(jnp.bfloat16).astype(jnp.float32)
    middle = (top - high).astype(jnp.bfloat16).astype(jnp.float32)
    low = top - high - middle
    lane = lax.broadcasted_iota(jnp.int32, (length, LANES), 1)
    row = lax.broadcasted_iota(jnp.int32, (length, LANES), 0)
    lane = lane - ((row >> (count.bit_length() - 1)) * GROUP + 3 * branch)
    parts = jnp.where(lane == 0, high, jnp.where(lane == 1, middle, jnp.where(lane == 2, low, 0.0)))
    return jnp.sum(parts.reshape(NEAR, count, LANES), axis=0)


def nearest(members, rows, dim, low, query, pairs):
    each = LANES // dim
    for side, (query_in, key_in, value_in) in members:
        core = (low ^ side) % 2
        query[core] = query_in
        for head in range(each):
            lanes = slice(head * dim, (head + 1) * dim)
            pairs[head, core] = jnp.concatenate([key_in[:, lanes], value_in[:, lanes]], axis=1)
    return [
        (
            query[:, :, head * dim : (head + 1) * dim].reshape(2 * rows, dim),
            pairs[head].reshape(2 * rows, LANES),
            0,
            None,
        )
        for head in range(each)
    ]


def nearest_out(top, accum):
    lane = lax.broadcasted_iota(jnp.int32, (1, LANES), 1)
    return jnp.where(lane == 0, top, accum).reshape(2, top.shape[0] // 2, LANES)


def raw_blocks(ref, rows, first=0):
    return tuple(ref[first + part * rows : first + (part + 1) * rows] for part in range(3))


def own_chip_kernel(sets, rows, dim, offset_ref, index_ref, own_ref, pair_ref, *refs):
    near_ref, pick_refs, query, pairs = refs[0], refs[1:3], *refs[3:]
    low = index_ref[0] % NEAR
    members = [(side, raw_blocks(ref, rows)) for side, ref in enumerate((own_ref, pair_ref))]
    blocks = [block[1:] for _, block in members]
    for pick, pick_ref in zip(far_picks(sets, rows, dim, low, offset_ref, blocks, [low, low]), pick_refs):
        pick_ref[...] = pick
    jobs = nearest(members, rows, dim, low, query, pairs)
    for head, (top, accum) in enumerate(attend(jobs, 4)):
        near_ref[head] = nearest_out(top, accum)


def local_kernel(rows, dim, offset_ref, index_ref, *refs):
    own_ref, core_ref, chip_ref, own_chip_ref, residual_ref, refs = *refs[:5], refs[5:]
    near_ref, far_ref, top_ref, picked_ref, residual_out = refs[:5]
    query, pairs, tight_pairs, tight_query = refs[5:]
    residual_out[...] = residual_ref[...]
    blocks = [raw_blocks(ref, rows) for ref in (own_ref, core_ref, chip_ref)]
    blocks.append(raw_blocks(chip_ref, rows, 3 * rows))
    each = LANES // dim
    low = index_ref[0] % NEAR
    chip = low // 2
    count = rows // 2
    left = lax.broadcasted_iota(jnp.int32, (1, LANES), 1) < dim
    selects = [
        selection(rows, range(1, BRANCHES), offset_ref, low * each + head) for head in range(each)
    ]
    for side in range(NEAR):
        query_in, key_in, value_in = blocks[side]
        both = [jnp.dot(select, query_in, preferred_element_type=jnp.float32) for select in selects]
        picked = jnp.where(left, both[0], both[1])
        tight_query[low ^ side] = picked[:count].astype(jnp.bfloat16)
        rest = picked[count:]
        rest = [rest, jnp.zeros((picked_ref.shape[1] - rest.shape[0], LANES), jnp.float32)]
        picked_ref[low ^ side] = jnp.concatenate(rest, axis=0).astype(jnp.bfloat16)
        for head in range(each):
            lanes = slice(head * dim, (head + 1) * dim)
            block = jnp.concatenate([key_in[:, lanes], value_in[:, lanes]], axis=1)
            block = jnp.dot(selects[head][:count], block, preferred_element_type=jnp.float32)
            tight_pairs[head, low ^ side] = block.astype(jnp.bfloat16)
    members = [(side, blocks[side]) for side in range(2, NEAR)]
    jobs = nearest(members, rows, dim, low, query, pairs)
    for head in range(each):
        near_ref[head, pl.ds(chip * 2, 2)] = own_chip_ref[head]
        jobs.append(
            (
                tight_query[:, :, head * dim : (head + 1) * dim].reshape(NEAR * count, dim),
                tight_pairs[head].reshape(NEAR * count, LANES),
                0,
                None,
            )
        )
    results = attend(jobs, 4)
    for head in range(each):
        near_ref[head, pl.ds((chip ^ 1) * 2, 2)] = nearest_out(*results[head])
        top, accum = results[each + head]
        far_ref[head] = accum.reshape(NEAR, count, LANES)
        top_ref[head] = top_lanes(top, count, 1)


def far_work(sets, rows, dim, index_ref, far_refs, query_ref, far, tops):
    each = LANES // dim
    group = index_ref[0] // NEAR
    starts, _ = part_rows(rows, range(1, BRANCHES))
    query_at, _ = part_rows(rows, range(2, BRANCHES))
    at, _ = set_rows(sets, rows, each)
    jobs, slots = [], []
    for number, (span, branches) in enumerate(sets):
        place = group % span
        first = at[number]
        for branch in branches:
            count = rows // 2**branch
            length = NEAR * count
            col = lax.broadcasted_iota(jnp.int32, (1, span * length), 1)
            step = span - 1 - (col >> (length.bit_length() - 1))
            columns = jnp.where((step == 0) | ((place ^ step) < place), col, 1 << 30)
            queries = query_ref[:, query_at[branch] : query_at[branch] + even(count), :]
            blocks = []
            for far_step in reversed(range(span)):
                skip = first - at[first_set(sets, far_step)]
                blocks.append(far_refs[far_step][:, skip : skip + each * count, :])
            if count % 16:
                queries = queries.astype(jnp.float32)[:, :count]
                blocks = [block.astype(jnp.float32) for block in blocks]
            for head in range(each):
                pairs = [block[:, head * count : (head + 1) * count].reshape(length, LANES) for block in blocks]
                pairs = jnp.concatenate(pairs, axis=0).astype(jnp.bfloat16)
                query = queries[:, :, head * dim : (head + 1) * dim].reshape(length, dim)
                jobs.append((query.astype(jnp.bfloat16), pairs, (span - 1) * length, columns))
                slots.append((branch, head, count))
            first += each * count
    for (branch, head, count), (top, accum) in zip(slots, attend(jobs, 2 * len(jobs))):
        into = slice(starts[branch], starts[branch] + count)
        far[head, :, into, :] = accum.reshape(NEAR, count, LANES)
        tops[head, into, :] = top_lanes(top, count, branch)


def hold_kernel(block_ref, ahead_ref, out_ref):
    out_ref[...] = block_ref[...]


def finish_kernel(sets, rows, dim, offset_ref, index_ref, *refs):
    steps = max(span for span, _ in sets)
    far_refs, refs = refs[:steps], refs[steps:]
    query_ref, near_ref, tight_ref, tight_top_ref, refs = *refs[:4], refs[4:]
    out_refs, far, tops, mixed_ref = refs[:NEAR], *refs[NEAR:]
    each = LANES // dim
    low = index_ref[0] % NEAR
    starts, used = part_rows(rows, range(1, BRANCHES))
    tight = rows // 2
    for head in range(each):
        far[head, :, :tight, :] = tight_ref[head]
        far[head, :, used:, :] = jnp.zeros((NEAR, rows - used, LANES), jnp.float32)
        tops[head, :tight, :] = tight_top_ref[head]
        tops[head, used:, :] = jnp.zeros((rows - used, LANES), jnp.float32)
    far_work(sets, rows, dim, index_ref, far_refs, query_ref, far, tops)

    lane = lax.broadcasted_iota(jnp.int32, (1, LANES), 1)
    inside = lane % GROUP
    column = lax.broadcasted_iota(jnp.int32, (1, rows), 1)
    row = lax.broadcasted_iota(jnp.int32, (rows, 1), 0)
    row_wide = lax.broadcasted_iota(jnp.int32, (rows, rows), 0)
    column_wide = lax.broadcasted_iota(jnp.int32, (rows, rows), 1)
    row_lane = lax.broadcasted_iota(jnp.int32, (rows, LANES), 0)

    def along(start_of, value_of, fill):
        result = jnp.full(start_of.shape, fill, jnp.int32)
        for branch in range(1, BRANCHES):
            result = jnp.where(start_of >= starts[branch], value_of(branch), result)
        return result

    masks = jnp.zeros((1, LANES), jnp.int32)
    for branch in range(1, BRANCHES):
        masks = jnp.where(inside == 3 * branch, 2**branch - 1, masks)
    own_lane = along(row, lambda branch: 3 * branch, 0)

    def turned(array, lanes):
        return pltpu.roll(array, lanes % LANES, 1)

    heads = range(each)
    spreads, gathers, covered = [], [], []
    for head in heads:
        offsets = {
            branch: offset_ref[branch, low * each + head] & (2**branch - 1)
            for branch in range(1, BRANCHES)
        }
        chosen = jnp.where(inside == 0, 0, 1)
        for branch in range(1, BRANCHES):
            chosen = jnp.where(inside == 3 * branch, offsets[branch], chosen)

        def position_of(slot):
            rate = along(slot, lambda branch: 2**branch, 0)
            inner = slot - along(slot, lambda branch: starts[branch], 0)
            return inner * rate + along(slot, lambda branch: offsets[branch], 0)

        spreads.append(jnp.where(row_wide == position_of(column), 1.0, 0.0).astype(jnp.bfloat16))
        gathers.append(jnp.where(column_wide == position_of(row), 1.0, 0.0).astype(jnp.bfloat16))
        covered.append((row_lane & masks) == chosen)
    stats = [
        jnp.dot(spreads[head], tops[head].astype(jnp.bfloat16), preferred_element_type=jnp.float32)
        for head in heads
    ]
    stats = [block + turned(block, -1) + turned(block, -2) for block in stats]
    for member in range(NEAR):
        stats = [
            jnp.where(lane == GROUP * member, near_ref[head, member][:, 0:1], stats[head]) for head in heads
        ]
    stats = [jnp.where(covered[head], stats[head], masked_score) for head in heads]
    peaks = stats
    for step in (3, 6, 12):
        peaks = [jnp.maximum(peak, turned(peak, -step)) for peak in peaks]
    peaks = [jnp.where(inside == 0, peak, masked_score) for peak in peaks]
    for step in (3, 6, 12):
        peaks = [jnp.maximum(peak, turned(peak, step)) for peak in peaks]
    weight = [
        jnp.where(block > 0.5 * masked_score, jnp.exp(block - peak), 0.0)
        for block, peak in zip(stats, peaks)
    ]
    weights = [
        jnp.dot(gathers[head], weight[head].astype(jnp.bfloat16), preferred_element_type=jnp.float32)
        for head in heads
    ]
    scaled = [[] for _ in heads]
    for member in range(NEAR):
        for head in heads:
            picked = jnp.where(lane == own_lane + GROUP * member, weights[head], 0.0)
            block = far[head, member] * jnp.sum(picked, axis=1, keepdims=True)
            rest = block - block.astype(jnp.bfloat16).astype(jnp.float32)
            scaled[head].append(jnp.where(lane == 0, rest, block).astype(jnp.bfloat16))
    added = [
        jnp.dot(spreads[head], jnp.concatenate(scaled[head], axis=1), preferred_element_type=jnp.float32)
        for head in heads
    ]
    halves = [[] for _ in heads]
    for member in range(NEAR):
        for head in heads:
            block = added[head][:, member * LANES : (member + 1) * LANES]
            own = weight[head][:, GROUP * member : GROUP * member + 1]
            total = block + own * near_ref[head, member]
            below = total[:, 1:2] + block[:, 0:1]
            halves[head].append(total[:, dim:] * (1.0 / below))
    for member in range(NEAR):
        pair = [mixed[member] for mixed in halves]
        mixed_ref[member] = jnp.concatenate(pair, axis=1).astype(jnp.bfloat16)
    for side in range(NEAR):
        out_refs[side][...] = mixed_ref[low ^ side]


def lay_out(low, block_refs, part, mix_ref):
    for side, ref in enumerate(block_refs):
        lanes = pl.ds(pl.multiple_of((low ^ side) * LANES, LANES), LANES)
        mix_ref[:, lanes] = ref[part, :]


def own_kernel(index_ref, residual_ref, other_residual_ref, weight_ref, *refs):
    block_refs, out_ref, mix_ref = refs[:NEAR], refs[NEAR], refs[NEAR + 1]
    rows, half = residual_ref.shape
    mine = pl.ds(pl.multiple_of(index_ref[1] * half, LANES), half)
    theirs = pl.ds(pl.multiple_of((1 - index_ref[1]) * half, LANES), half)
    lay_out(index_ref[0] % NEAR, block_refs, slice(0, rows), mix_ref)
    out_ref[...] = jnp.dot(mix_ref[...], weight_ref[...], preferred_element_type=jnp.float32)
    out_ref[:, mine] += residual_ref[...].astype(jnp.float32)
    out_ref[:, theirs] += other_residual_ref[...].astype(jnp.float32)


def block_kernel(part, index_ref, own_ref, *refs):
    block_refs, refs = refs[:NEAR], refs[NEAR:]
    first_weight_ref, second_weight_ref, gain_ref, gate_ref, up_ref, down_ref = refs[:6]
    theirs_ref, mine_ref, hidden_ref, act_ref, mix_ref = refs[6:]
    half = theirs_ref.shape[1]
    mine = pl.ds(pl.multiple_of(index_ref[1] * half, LANES), half)
    theirs = pl.ds(pl.multiple_of((1 - index_ref[1]) * half, LANES), half)
    count = first_weight_ref.shape[0]
    core = index_ref[0] % 2
    lay_out(index_ref[0] % NEAR, block_refs, part, mix_ref)
    hidden = own_ref[part, :]
    for place, weight_ref in ((core, first_weight_ref), (1 - core, second_weight_ref)):
        lanes = pl.ds(pl.multiple_of(place * count, LANES), count)
        hidden += jnp.dot(mix_ref[:, lanes], weight_ref[...], preferred_element_type=jnp.float32)
    hidden_ref[...] = hidden
    inverse = lax.rsqrt(jnp.mean(hidden * hidden, axis=1, keepdims=True) + 1e-05)
    normed = (hidden * inverse * gain_ref[...]).astype(jnp.bfloat16)
    step = 256
    for first in range(0, act_ref.shape[1], step):
        gate = jnp.dot(normed, gate_ref[:, first : first + step], preferred_element_type=jnp.float32)
        up = jnp.dot(normed, up_ref[:, first : first + step], preferred_element_type=jnp.float32)
        act_ref[:, first : first + step] = (gate / (1.0 + jnp.exp(-gate)) * up).astype(jnp.bfloat16)
    act = act_ref[...]
    theirs_ref[...] = jnp.dot(act, down_ref[:, theirs], preferred_element_type=jnp.float32).astype(
        jnp.bfloat16
    )
    mine_ref[...] = hidden_ref[:, mine] + jnp.dot(
        act, down_ref[:, mine], preferred_element_type=jnp.float32
    )


def add_kernel(*refs):
    count = (len(refs) - 1) // 2
    out_ref = refs[-1]
    for number in range(count):
        mine, theirs = refs[number], refs[count + number]
        step = mine.shape[0]
        out_ref[number * step : (number + 1) * step, :] = (
            mine[...] + theirs[...].astype(jnp.float32)
        ).astype(out_ref.dtype)


def call(kernel, out_shape, smem, operands, micros, scratch=(), vmem=8):
    specs = [
        pl.BlockSpec(memory_space=pltpu.SMEM if number < smem else pltpu.VMEM)
        for number in range(len(operands))
    ]
    return pl.pallas_call(
        kernel,
        out_shape=out_shape,
        in_specs=specs,
        out_specs=jax.tree.map(lambda _: pl.BlockSpec(memory_space=pltpu.VMEM), out_shape),
        scratch_shapes=list(scratch),
        compiler_params=pltpu.CompilerParams(vmem_limit_bytes=vmem * MIB),
        cost_estimate=pl.CostEstimate(
            flops=int(micros * PEAK_FLOPS / 1e6), bytes_accessed=0, transcendentals=0
        ),
    )(*operands)


def shards(
    residual_in,
    queries,
    keys,
    values,
    head_offset,
    out_weight,
    norm_gain,
    gate_weight,
    up_weight,
    down_weight,
):
    rows, cols = queries.shape
    heads = head_offset.shape[1]
    dim = cols // heads
    each = heads // NEAR
    seq_count = lax.axis_size("seq")
    scale = 1.0 / math.sqrt(dim)
    sets = far_sets(seq_count, rows)
    index = jnp.stack([lax.axis_index("seq"), lax.axis_index("tp")]).astype(jnp.int32)
    bf16 = jnp.bfloat16

    def shape(*sizes, dtype=bf16):
        return jax.ShapeDtypeStruct(sizes, dtype)

    def across(block, distance):
        if distance == 0:
            return block
        return lax.ppermute(block, "seq", [(i, i ^ distance) for i in range(seq_count)])

    swap = [(0, 1), (1, 0)]
    half = out_weight.shape[0] // 2
    part = lax.dynamic_slice_in_dim(out_weight, lax.axis_index("seq") % 2 * half, half)
    part = lax.ppermute(part, "tp", swap)
    other_weights = (part, across(part, 1))

    source = jnp.concatenate([queries, keys, values], axis=0)
    _, tall = part_rows(rows, range(2, BRANCHES))
    first, second, own, core, chip = call(
        functools.partial(split_kernel, sets, scale, dim),
        [shape(each * tall, LANES)] * 2 + [shape(part * rows, LANES) for part in (3, 6, 3)],
        2,
        (head_offset, index, source),
        1.0,
        vmem=12,
    )
    wide = [across(first, 2), across(second, 3)]
    core = across(core, 1)
    own_chip, *picks = call(
        functools.partial(own_chip_kernel, sets, rows, dim),
        [shape(each, 2, rows, LANES, dtype=jnp.float32)] + [shape(each * tall, LANES)] * 2,
        2,
        (head_offset, index, own, core),
        2.0,
        [pltpu.VMEM((2, rows, LANES), bf16), pltpu.VMEM((each, 2, rows, LANES), bf16)],
        vmem=12,
    )
    at, all_rows = set_rows(sets, rows, each)
    *turned, relay = call(
        functools.partial(turn_kernel, at),
        [shape(NEAR, all_rows - first, LANES) for first in at] + [shape(6 * rows, LANES)],
        1,
        (index, *picks, *wide, chip, core),
        0.3,
    )
    chip = across(relay, 2)
    far = [
        across(turned[first_set(sets, step)], NEAR * step)
        for step in range(max(span for span, _ in sets))
    ]

    near, tight_done, tight_top, picked_queries, residual = call(
        functools.partial(local_kernel, rows, dim),
        [
            shape(each, NEAR, rows, LANES, dtype=jnp.float32),
            shape(each, NEAR, rows // 2, LANES, dtype=jnp.float32),
            shape(each, rows // 2, LANES, dtype=jnp.float32),
            shape(NEAR, even(tall), LANES),
            shape(rows, cols),
        ],
        2,
        (head_offset, index, own, core, chip, own_chip, residual_in),
        4.0,
        [
            pltpu.VMEM((2, rows, LANES), bf16),
            pltpu.VMEM((each, 2, rows, LANES), bf16),
            pltpu.VMEM((each, NEAR, rows // 2, LANES), bf16),
            pltpu.VMEM((NEAR, rows // 2, LANES), bf16),
        ],
        vmem=12,
    )
    mixes = call(
        functools.partial(finish_kernel, sets, rows, dim),
        [shape(rows, LANES)] * NEAR,
        2,
        (head_offset, index, *far, picked_queries, near, tight_done, tight_top),
        6.0,
        [
            pltpu.VMEM((each, NEAR, rows, LANES), jnp.float32),
            pltpu.VMEM((each, rows, LANES), jnp.float32),
            pltpu.VMEM((NEAR, rows, LANES), bf16),
        ],
        vmem=16,
    )
    mixes = [across(block, step) for step, block in enumerate(mixes)]
    held = call(hold_kernel, shape(rows, LANES), 0, (mixes[0], other_weights[1]), 0.2)
    other_mixes = [lax.ppermute(block, "tp", swap) for block in (held, *mixes[1:])]

    other_residual = lax.ppermute(residual, "tp", swap)
    width = norm_gain.shape[0]
    mine, theirs = [], []
    own = call(
        own_kernel,
        shape(rows, width, dtype=jnp.float32),
        1,
        (index, residual_in, other_residual, out_weight, *mixes),
        1.2,
        [pltpu.VMEM((rows, cols), bf16)],
    )
    step = rows // CHUNKS
    for number in range(CHUNKS):
        part = slice(number * step, (number + 1) * step)
        send, keep = call(
            functools.partial(block_kernel, part),
            [shape(step, cols), shape(step, cols, dtype=jnp.float32)],
            1,
            (
                index,
                own,
                *other_mixes,
                *other_weights,
                norm_gain.reshape(1, width),
                gate_weight,
                up_weight,
                down_weight,
            ),
            2.0,
            [
                pltpu.VMEM((step, width), jnp.float32),
                pltpu.VMEM((step, gate_weight.shape[1]), bf16),
                pltpu.VMEM((step, cols), bf16),
            ],
        )
        mine.append(keep)
        theirs.append(lax.ppermute(send, "tp", swap))
    return call(add_kernel, shape(rows, cols), 0, (*mine, *theirs), 0.8)


def solution(mesh):
    placed = (
        P("seq", "tp"),
        P("seq", "tp"),
        P("seq", "tp"),
        P("seq", "tp"),
        P(None, "tp"),
        P("tp", None),
        P(),
        P(None, "tp"),
        P(None, "tp"),
        P("tp", None),
    )
    return jax.shard_map(
        shards, mesh=mesh, in_specs=placed, out_specs=P("seq", "tp"), check_vma=False
    )
```

```python
import functools
import math

import jax
import jax.numpy as jnp
from jax import lax
from jax.experimental import pallas as pl
from jax.experimental.pallas import tpu as pltpu
from jax.sharding import PartitionSpec as P

BRANCHES = 6
LANES = 128
NEAR = 4
GROUP = LANES // NEAR
PEAK_FLOPS = 1153.5e12
MIB = 1024 * 1024
CHUNKS = 2

masked_score = -1e30


def part_rows(rows, branches):
    first, at = 0, {}
    for branch in branches:
        at[branch] = first
        first += rows // 2**branch
    return at, first


def far_sets(seq_count, rows):
    top_bits = min(seq_count.bit_length() - 1, BRANCHES)
    sets = {}
    for branch in range(2, BRANCHES):
        sets.setdefault(2 ** min(branch + 1, top_bits) // NEAR, []).append(branch)
    return sorted(sets.items())


def set_rows(sets, rows, each):
    first, at = 0, []
    for _, branches in sets:
        at.append(first)
        first += each * sum(rows // 2**branch for branch in branches)
    return at, first


def first_set(sets, step):
    return min(number for number, (span, _) in enumerate(sets) if span > step)


def even(count):
    return -(-count // 16) * 16


def mask_select(rows, branch, offset):
    rate = 2**branch
    count = rows // rate
    row = lax.broadcasted_iota(jnp.int32, (count, rows), 0)
    col = lax.broadcasted_iota(jnp.int32, (count, rows), 1)
    return jnp.where(col == row * rate + (offset & (rate - 1)), 1.0, 0.0)


def selection(rows, branches, offset_ref, head):
    select = [mask_select(rows, branch, offset_ref[branch, head]) for branch in branches]
    return jnp.concatenate(select, axis=0).astype(jnp.bfloat16)


def far_picks(sets, rows, dim, blocks, selects):
    each = LANES // dim
    far_branches = range(2, BRANCHES)
    starts, _ = part_rows(rows, far_branches)
    picked = []
    for (key, value), mine in zip(blocks, selects):
        for head in range(each):
            lanes = slice(head * dim, (head + 1) * dim)
            pairs = jnp.concatenate([key[:, lanes], value[:, lanes]], axis=1)
            picked.append(jnp.dot(mine[head], pairs, preferred_element_type=jnp.float32))
    outs = []
    for number in range(len(blocks)):
        parts = []
        for _, branches in sets:
            for branch in branches:
                first, last = starts[branch], starts[branch] + rows // 2**branch
                parts += [picked[number * each + head][first:last] for head in range(each)]
        outs.append(jnp.concatenate(parts, axis=0).astype(jnp.bfloat16))
    return outs


def split_kernel(sets, scale, dim, offset_ref, index_ref, source_ref, *out_refs):
    wide_refs, own_ref, core_ref, chip_ref = out_refs[:2], *out_refs[2:]
    rows = source_ref.shape[0] // 3
    low = index_ref[0] % NEAR
    all_lanes = [
        pl.ds(pl.multiple_of((low ^ side) * LANES, LANES), LANES) for side in range(NEAR)
    ]
    blocks = [
        (source_ref[rows : 2 * rows, lanes], source_ref[2 * rows :, lanes]) for lanes in all_lanes[2:]
    ]
    each = LANES // dim
    selects = [
        [selection(rows, range(2, BRANCHES), offset_ref, (low ^ side) * each + head) for head in range(each)]
        for side in (2, 3)
    ]
    picks = far_picks(sets, rows, dim, blocks, selects)
    for pick, wide_ref in zip(picks, wide_refs):
        wide_ref[...] = pick
    for side, lanes in enumerate(all_lanes):
        ref, first = ((own_ref, 0), (core_ref, 0), (chip_ref, 0), (core_ref, 3 * rows))[side]
        ref[first : first + rows] = source_ref[:rows, lanes] * jnp.asarray(scale, jnp.bfloat16)
        ref[first + rows : first + 3 * rows] = source_ref[rows:, lanes]


def turn_kernel(at, index_ref, *refs):
    in_refs, out_refs = refs[:NEAR], refs[NEAR + 1 : -1]
    low = index_ref[0] % NEAR
    for side in range(NEAR):
        for first, out_ref in zip(at, out_refs):
            out_ref[low ^ side] = in_refs[side][first:, :]


def attend(jobs, batch):
    dim = jobs[0][0].shape[1]
    lane = lax.broadcasted_iota(jnp.int32, (1, LANES), 1)
    keys = [pairs[:, :dim] for _, pairs, _, _ in jobs]
    values = [jnp.where(lane < dim, jnp.ones_like(pairs), pairs) for _, pairs, _, _ in jobs]
    pieces = []
    for number, (query, _, _, _) in enumerate(jobs):
        block = min(128, query.shape[0])
        pieces += [(start, number, block) for start in range(0, query.shape[0], block)]
    pieces.sort(key=lambda piece: piece[0])
    done = {}
    for at in range(0, len(pieces), batch):
        now = pieces[at : at + batch]
        scores = []
        for start, number, block in now:
            query, _, before, _ = jobs[number]
            scores.append(
                lax.dot_general(
                    query[start : start + block],
                    keys[number][: before + start + block],
                    (((1,), (1,)), ((), ())),
                    preferred_element_type=jnp.float32,
                )
            )
        masked = []
        for (start, number, block), score in zip(now, scores):
            _, _, before, columns = jobs[number]
            end = before + start + block
            if before == 0 and block == 128:
                row = lax.broadcasted_iota(jnp.int32, (block, block), 0)
                col = lax.broadcasted_iota(jnp.int32, (block, block), 1)
                last = jnp.where(col <= row, score[:, start:], masked_score)
                masked.append(jnp.concatenate([score[:, :start], last], axis=1) if start else last)
            else:
                row = lax.broadcasted_iota(jnp.int32, (block, end), 0)
                allowed = columns[:, :end] <= row + (before + start)
                masked.append(jnp.where(allowed, score, masked_score))
        tops = [jnp.max(score, axis=1, keepdims=True) for score in masked]
        weights = [jnp.exp(score - top).astype(jnp.bfloat16) for score, top in zip(masked, tops)]
        for piece, weight, top in zip(now, weights, tops):
            start, number, block = piece
            end = jobs[number][2] + start + block
            accum = jnp.dot(weight, values[number][:end], preferred_element_type=jnp.float32)
            done.setdefault(number, []).append((top, accum))
    return [
        tuple(jnp.concatenate(column, axis=0) for column in zip(*done[number]))
        for number in range(len(jobs))
    ]


def top_lanes(top, count, branch):
    length = top.shape[0]
    high = top.astype(jnp.bfloat16).astype(jnp.float32)
    middle = (top - high).astype(jnp.bfloat16).astype(jnp.float32)
    low = top - high - middle
    lane = lax.broadcasted_iota(jnp.int32, (length, LANES), 1)
    row = lax.broadcasted_iota(jnp.int32, (length, LANES), 0)
    lane = lane - ((row >> (count.bit_length() - 1)) * GROUP + 3 * branch)
    parts = jnp.where(lane == 0, high, jnp.where(lane == 1, middle, jnp.where(lane == 2, low, 0.0)))
    return jnp.sum(parts.reshape(NEAR, count, LANES), axis=0)


def nearest(members, rows, dim, low, query, pairs):
    each = LANES // dim
    for side, (query_in, key_in, value_in) in members:
        core = (low ^ side) % 2
        query[core] = query_in
        for head in range(each):
            lanes = slice(head * dim, (head + 1) * dim)
            pairs[head, core] = jnp.concatenate([key_in[:, lanes], value_in[:, lanes]], axis=1)
    return [
        (
            query[:, :, head * dim : (head + 1) * dim].reshape(2 * rows, dim),
            pairs[head].reshape(2 * rows, LANES),
            0,
            None,
        )
        for head in range(each)
    ]


def nearest_out(top, accum):
    lane = lax.broadcasted_iota(jnp.int32, (1, LANES), 1)
    return jnp.where(lane == 0, top, accum).reshape(2, top.shape[0] // 2, LANES)


def raw_blocks(ref, rows, first=0):
    return tuple(ref[first + part * rows : first + (part + 1) * rows] for part in range(3))


def local_picks(rows, dim, block, select_ref):
    query, key, value = block
    each = LANES // dim
    left = lax.broadcasted_iota(jnp.int32, (1, LANES), 1) < dim
    both = [jnp.dot(select_ref[head], query, preferred_element_type=jnp.float32) for head in range(each)]
    pairs = []
    for head in range(each):
        lanes = slice(head * dim, (head + 1) * dim)
        pair = jnp.concatenate([key[:, lanes], value[:, lanes]], axis=1)
        pair = jnp.dot(select_ref[head, : rows // 2], pair, preferred_element_type=jnp.float32)
        pairs.append(pair.astype(jnp.bfloat16))
    return jnp.where(left, both[0], both[1]).astype(jnp.bfloat16), pairs


def own_chip_kernel(sets, rows, dim, offset_ref, index_ref, own_ref, pair_ref, chip_ref, *refs):
    near_ref, pick_refs, relay_ref = refs[0], refs[1:3], refs[3]
    select_ref, spread_ref, picked_ref, tight_ref, query, pairs = refs[4:]
    half = chip_ref.shape[0]
    relay_ref[:half] = chip_ref[...]
    relay_ref[half:] = pair_ref[half:]
    each = LANES // dim
    low = index_ref[0] % NEAR
    starts, used = part_rows(rows, range(1, BRANCHES))
    column = lax.broadcasted_iota(jnp.int32, (1, rows), 1)
    row_wide = lax.broadcasted_iota(jnp.int32, (rows, rows), 0)
    for head in range(each):
        select = [mask_select(rows, b, offset_ref[b, low * each + head]) for b in range(1, BRANCHES)]
        select.append(jnp.zeros((rows - used, rows), jnp.float32))
        select_ref[head] = jnp.concatenate(select, axis=0).astype(jnp.bfloat16)
        target = jnp.full((1, rows), -1, jnp.int32)
        for branch in range(1, BRANCHES):
            rate = 2**branch
            offset = offset_ref[branch, low * each + head] & (rate - 1)
            target = jnp.where(
                column >= starts[branch], (column - starts[branch]) * rate + offset, target
            )
        spread_ref[head] = jnp.where(row_wide == target, 1.0, 0.0).astype(jnp.bfloat16)
    members = [(side, raw_blocks(ref, rows)) for side, ref in enumerate((own_ref, pair_ref))]
    selects = [select_ref[head, rows // 2 : used] for head in range(each)]
    blocks = [block[1:] for _, block in members]
    for pick, pick_ref in zip(far_picks(sets, rows, dim, blocks, [selects, selects]), pick_refs):
        pick_ref[...] = pick
    for side, block in members:
        picked, tight = local_picks(rows, dim, block, select_ref)
        core = (low ^ side) % 2
        picked_ref[core] = picked
        for head in range(each):
            tight_ref[head, core] = tight[head]
    jobs = nearest(members, rows, dim, low, query, pairs)
    for head, (top, accum) in enumerate(attend(jobs, 4)):
        near_ref[head] = nearest_out(top, accum)


def local_kernel(rows, dim, index_ref, *refs):
    chip_ref, own_chip_ref, select_ref, own_picked_ref, own_tight_ref, residual_ref = refs[:6]
    near_ref, far_ref, top_ref, picked_ref, residual_out = refs[6:11]
    query, pairs, tight_pairs, tight_query = refs[11:]
    residual_out[...] = residual_ref[...]
    each = LANES // dim
    low = index_ref[0] % NEAR
    chip = low // 2
    count = rows // 2
    blocks = {side: raw_blocks(chip_ref, rows, 3 * rows * (side - 2)) for side in (2, 3)}
    for core in range(2):
        tight_query[chip * 2 + core] = own_picked_ref[core, :count]
        picked_ref[chip * 2 + core] = own_picked_ref[core, count:]
        for head in range(each):
            tight_pairs[head, chip * 2 + core] = own_tight_ref[head, core]
    for side in (2, 3):
        picked, tight = local_picks(rows, dim, blocks[side], select_ref)
        tight_query[low ^ side] = picked[:count]
        picked_ref[low ^ side] = picked[count:]
        for head in range(each):
            tight_pairs[head, low ^ side] = tight[head]
    members = [(side, blocks[side]) for side in range(2, NEAR)]
    jobs = nearest(members, rows, dim, low, query, pairs)
    for head in range(each):
        near_ref[head, pl.ds(chip * 2, 2)] = own_chip_ref[head]
        jobs.append(
            (
                tight_query[:, :, head * dim : (head + 1) * dim].reshape(NEAR * count, dim),
                tight_pairs[head].reshape(NEAR * count, LANES),
                0,
                None,
            )
        )
    results = attend(jobs, 4)
    for head in range(each):
        near_ref[head, pl.ds((chip ^ 1) * 2, 2)] = nearest_out(*results[head])
        top, accum = results[each + head]
        far_ref[head] = accum.reshape(NEAR, count, LANES)
        top_ref[head] = top_lanes(top, count, 1)


def far_work(sets, rows, dim, index_ref, far_refs, query_ref, far, tops):
    each = LANES // dim
    group = index_ref[0] // NEAR
    starts, _ = part_rows(rows, range(1, BRANCHES))
    query_at, _ = part_rows(rows, range(2, BRANCHES))
    at, _ = set_rows(sets, rows, each)
    jobs, slots = [], []
    for number, (span, branches) in enumerate(sets):
        place = group % span
        first = at[number]
        for branch in branches:
            count = rows // 2**branch
            length = NEAR * count
            col = lax.broadcasted_iota(jnp.int32, (1, span * length), 1)
            step = span - 1 - (col >> (length.bit_length() - 1))
            columns = jnp.where((step == 0) | ((place ^ step) < place), col, 1 << 30)
            queries = query_ref[:, query_at[branch] : query_at[branch] + even(count), :]
            blocks = []
            for far_step in reversed(range(span)):
                skip = first - at[first_set(sets, far_step)]
                blocks.append(far_refs[far_step][:, skip : skip + each * count, :])
            if count % 16:
                queries = queries.astype(jnp.float32)[:, :count]
                blocks = [block.astype(jnp.float32) for block in blocks]
            for head in range(each):
                pairs = [block[:, head * count : (head + 1) * count].reshape(length, LANES) for block in blocks]
                pairs = jnp.concatenate(pairs, axis=0).astype(jnp.bfloat16)
                query = queries[:, :, head * dim : (head + 1) * dim].reshape(length, dim)
                jobs.append((query.astype(jnp.bfloat16), pairs, (span - 1) * length, columns))
                slots.append((branch, head, count))
            first += each * count
    for (branch, head, count), (top, accum) in zip(slots, attend(jobs, 2 * len(jobs))):
        into = slice(starts[branch], starts[branch] + count)
        far[head, :, into, :] = accum.reshape(NEAR, count, LANES)
        tops[head, into, :] = top_lanes(top, count, branch)


def finish_kernel(sets, rows, dim, offset_ref, index_ref, *refs):
    steps = max(span for span, _ in sets)
    far_refs, refs = refs[:steps], refs[steps:]
    query_ref, near_ref, tight_ref, tight_top_ref, select_ref, spread_ref, refs = *refs[:6], refs[6:]
    out_refs, far, tops, mixed_ref = refs[:NEAR], *refs[NEAR:]
    each = LANES // dim
    low = index_ref[0] % NEAR
    starts, used = part_rows(rows, range(1, BRANCHES))
    tight = rows // 2
    for head in range(each):
        far[head, :, :tight, :] = tight_ref[head]
        far[head, :, used:, :] = jnp.zeros((NEAR, rows - used, LANES), jnp.float32)
        tops[head, :tight, :] = tight_top_ref[head]
        tops[head, used:, :] = jnp.zeros((rows - used, LANES), jnp.float32)
    far_work(sets, rows, dim, index_ref, far_refs, query_ref, far, tops)

    lane = lax.broadcasted_iota(jnp.int32, (1, LANES), 1)
    inside = lane % GROUP
    row = lax.broadcasted_iota(jnp.int32, (rows, 1), 0)
    row_lane = lax.broadcasted_iota(jnp.int32, (rows, LANES), 0)

    def along(start_of, value_of, fill):
        result = jnp.full(start_of.shape, fill, jnp.int32)
        for branch in range(1, BRANCHES):
            result = jnp.where(start_of >= starts[branch], value_of(branch), result)
        return result

    masks = jnp.zeros((1, LANES), jnp.int32)
    for branch in range(1, BRANCHES):
        masks = jnp.where(inside == 3 * branch, 2**branch - 1, masks)
    own_lane = along(row, lambda branch: 3 * branch, 0)

    def turned(array, lanes):
        return pltpu.roll(array, lanes % LANES, 1)

    heads = range(each)
    covered = []
    for head in heads:
        offsets = {
            branch: offset_ref[branch, low * each + head] & (2**branch - 1)
            for branch in range(1, BRANCHES)
        }
        chosen = jnp.where(inside == 0, 0, 1)
        for branch in range(1, BRANCHES):
            chosen = jnp.where(inside == 3 * branch, offsets[branch], chosen)
        covered.append((row_lane & masks) == chosen)
    stats = [
        jnp.dot(spread_ref[head], tops[head].astype(jnp.bfloat16), preferred_element_type=jnp.float32)
        for head in heads
    ]
    stats = [block + turned(block, -1) + turned(block, -2) for block in stats]
    for member in range(NEAR):
        stats = [
            jnp.where(lane == GROUP * member, near_ref[head, member][:, 0:1], stats[head]) for head in heads
        ]
    stats = [jnp.where(covered[head], stats[head], masked_score) for head in heads]
    peaks = stats
    for step in (3, 6, 12):
        peaks = [jnp.maximum(peak, turned(peak, -step)) for peak in peaks]
    peaks = [jnp.where(inside == 0, peak, masked_score) for peak in peaks]
    for step in (3, 6, 12):
        peaks = [jnp.maximum(peak, turned(peak, step)) for peak in peaks]
    weight = [
        jnp.where(block > 0.5 * masked_score, jnp.exp(block - peak), 0.0)
        for block, peak in zip(stats, peaks)
    ]
    weight = [block.astype(jnp.bfloat16) for block in weight]
    weights = [
        jnp.dot(select_ref[head], weight[head], preferred_element_type=jnp.float32) for head in heads
    ]
    from_lane = lax.broadcasted_iota(jnp.int32, (LANES, NEAR * LANES), 0)
    to_member = lax.broadcasted_iota(jnp.int32, (LANES, NEAR * LANES), 1) >> (LANES.bit_length() - 1)
    group = GROUP.bit_length() - 1
    any_lane = jnp.where(from_lane >> group == to_member, 1.0, 0.0).astype(jnp.bfloat16)
    first_lane = jnp.where(from_lane == to_member << group, 1.0, 0.0).astype(jnp.bfloat16)
    weights = [jnp.where(inside == own_lane, block, 0.0).astype(jnp.bfloat16) for block in weights]
    weights = [jnp.dot(block, any_lane, preferred_element_type=jnp.float32) for block in weights]
    owns = [jnp.dot(block, first_lane, preferred_element_type=jnp.float32) for block in weight]
    scaled = [[] for _ in heads]
    for member in range(NEAR):
        for head in heads:
            block = far[head, member] * weights[head][:, member * LANES : (member + 1) * LANES]
            rest = block - block.astype(jnp.bfloat16).astype(jnp.float32)
            scaled[head].append(jnp.where(lane == 0, rest, block).astype(jnp.bfloat16))
    added = [
        jnp.dot(spread_ref[head], jnp.concatenate(scaled[head], axis=1), preferred_element_type=jnp.float32)
        for head in heads
    ]
    halves = [[] for _ in heads]
    for member in range(NEAR):
        for head in heads:
            block = added[head][:, member * LANES : (member + 1) * LANES]
            own = owns[head][:, member * LANES : (member + 1) * LANES]
            total = block + own * near_ref[head, member]
            below = total[:, 1:2] + block[:, 0:1]
            halves[head].append(total[:, dim:] * (1.0 / below))
    for member in range(NEAR):
        pair = [mixed[member] for mixed in halves]
        mixed_ref[member] = jnp.concatenate(pair, axis=1).astype(jnp.bfloat16)
    for side in range(NEAR):
        out_refs[side][...] = mixed_ref[low ^ side]


def lay_out(low, block_refs, part, mix_ref):
    for side, ref in enumerate(block_refs):
        lanes = pl.ds(pl.multiple_of((low ^ side) * LANES, LANES), LANES)
        mix_ref[:, lanes] = ref[part, :]


def own_kernel(index_ref, residual_ref, other_residual_ref, weight_ref, *refs):
    block_refs, out_ref, mix_ref = refs[:NEAR], refs[NEAR], refs[NEAR + 1]
    rows, half = residual_ref.shape
    mine = pl.ds(pl.multiple_of(index_ref[1] * half, LANES), half)
    theirs = pl.ds(pl.multiple_of((1 - index_ref[1]) * half, LANES), half)
    lay_out(index_ref[0] % NEAR, block_refs, slice(0, rows), mix_ref)
    out_ref[...] = jnp.dot(mix_ref[...], weight_ref[...], preferred_element_type=jnp.float32)
    out_ref[:, mine] += residual_ref[...].astype(jnp.float32)
    out_ref[:, theirs] += other_residual_ref[...].astype(jnp.float32)


def block_kernel(part, index_ref, own_ref, *refs):
    block_refs, refs = refs[:NEAR], refs[NEAR:]
    first_weight_ref, second_weight_ref, gain_ref, gate_ref, up_ref, down_ref = refs[:6]
    theirs_ref, mine_ref, hidden_ref, act_ref, mix_ref = refs[6:]
    half = theirs_ref.shape[1]
    mine = pl.ds(pl.multiple_of(index_ref[1] * half, LANES), half)
    theirs = pl.ds(pl.multiple_of((1 - index_ref[1]) * half, LANES), half)
    count = first_weight_ref.shape[0]
    core = index_ref[0] % 2
    lay_out(index_ref[0] % NEAR, block_refs, part, mix_ref)
    hidden = own_ref[part, :]
    for place, weight_ref in ((core, first_weight_ref), (1 - core, second_weight_ref)):
        lanes = pl.ds(pl.multiple_of(place * count, LANES), count)
        hidden += jnp.dot(mix_ref[:, lanes], weight_ref[...], preferred_element_type=jnp.float32)
    hidden_ref[...] = hidden
    inverse = lax.rsqrt(jnp.mean(hidden * hidden, axis=1, keepdims=True) + 1e-05)
    normed = (hidden * inverse * gain_ref[...]).astype(jnp.bfloat16)
    step = 256
    for first in range(0, act_ref.shape[1], step):
        gate = jnp.dot(normed, gate_ref[:, first : first + step], preferred_element_type=jnp.float32)
        up = jnp.dot(normed, up_ref[:, first : first + step], preferred_element_type=jnp.float32)
        act_ref[:, first : first + step] = (gate / (1.0 + jnp.exp(-gate)) * up).astype(jnp.bfloat16)
    act = act_ref[...]
    theirs_ref[...] = jnp.dot(act, down_ref[:, theirs], preferred_element_type=jnp.float32).astype(
        jnp.bfloat16
    )
    mine_ref[...] = hidden_ref[:, mine] + jnp.dot(
        act, down_ref[:, mine], preferred_element_type=jnp.float32
    )


def add_kernel(*refs):
    count = (len(refs) - 1) // 2
    out_ref = refs[-1]
    for number in range(count):
        mine, theirs = refs[number], refs[count + number]
        step = mine.shape[0]
        out_ref[number * step : (number + 1) * step, :] = (
            mine[...] + theirs[...].astype(jnp.float32)
        ).astype(out_ref.dtype)


def call(kernel, out_shape, smem, operands, micros, scratch=(), vmem=8, passed=False):
    specs = [
        pl.BlockSpec(memory_space=pltpu.SMEM if number < smem else pltpu.VMEM)
        for number in range(len(operands))
    ]
    out_specs = jax.tree.map(lambda _: pl.BlockSpec(memory_space=pltpu.VMEM), out_shape)
    aliases = {}
    if passed:
        specs[-1] = out_specs[-1] = pl.BlockSpec(memory_space=pl.ANY)
        aliases = {len(specs) - 1: len(out_specs) - 1}
    return pl.pallas_call(
        kernel,
        out_shape=out_shape,
        in_specs=specs,
        out_specs=out_specs,
        input_output_aliases=aliases,
        scratch_shapes=list(scratch),
        compiler_params=pltpu.CompilerParams(vmem_limit_bytes=vmem * MIB),
        cost_estimate=pl.CostEstimate(
            flops=int(micros * PEAK_FLOPS / 1e6), bytes_accessed=0, transcendentals=0
        ),
    )(*operands)


def shards(
    residual_in,
    queries,
    keys,
    values,
    head_offset,
    out_weight,
    norm_gain,
    gate_weight,
    up_weight,
    down_weight,
):
    rows, cols = queries.shape
    heads = head_offset.shape[1]
    dim = cols // heads
    each = heads // NEAR
    seq_count = lax.axis_size("seq")
    scale = 1.0 / math.sqrt(dim)
    sets = far_sets(seq_count, rows)
    index = jnp.stack([lax.axis_index("seq"), lax.axis_index("tp")]).astype(jnp.int32)
    bf16 = jnp.bfloat16

    def shape(*sizes, dtype=bf16):
        return jax.ShapeDtypeStruct(sizes, dtype)

    def across(block, distance):
        if distance == 0:
            return block
        return lax.ppermute(block, "seq", [(i, i ^ distance) for i in range(seq_count)])

    swap = [(0, 1), (1, 0)]
    half = out_weight.shape[0] // 2
    part = lax.dynamic_slice_in_dim(out_weight, lax.axis_index("seq") % 2 * half, half)
    part = lax.ppermute(part, "tp", swap)
    other_weights = (part, across(part, 1))

    source = jnp.concatenate([queries, keys, values], axis=0)
    _, tall = part_rows(rows, range(2, BRANCHES))
    first, second, own, core, chip = call(
        functools.partial(split_kernel, sets, scale, dim),
        [shape(each * tall, LANES)] * 2 + [shape(part * rows, LANES) for part in (3, 6, 3)],
        2,
        (head_offset, index, source),
        1.0,
        vmem=12,
    )
    wide = [across(first, 2), across(second, 3)]
    core = across(core, 1)
    own_chip, first, second, relay, selects, spreads, own_picked, own_tight = call(
        functools.partial(own_chip_kernel, sets, rows, dim),
        [shape(each, 2, rows, LANES, dtype=jnp.float32)] + [shape(each * tall, LANES)] * 2
        + [shape(6 * rows, LANES)]
        + [shape(each, rows, rows)] * 2
        + [shape(2, rows, LANES), shape(each, 2, rows // 2, LANES)],
        2,
        (head_offset, index, own, core, chip),
        2.4,
        [pltpu.VMEM((2, rows, LANES), bf16), pltpu.VMEM((each, 2, rows, LANES), bf16)],
        vmem=12,
    )
    at, all_rows = set_rows(sets, rows, each)
    *turned, relay = call(
        functools.partial(turn_kernel, at),
        [shape(NEAR, all_rows - first, LANES) for first in at] + [shape(6 * rows, LANES)],
        1,
        (index, first, second, *wide, relay),
        0.3,
        passed=True,
    )
    chip = across(relay, 2)
    far = [
        across(turned[first_set(sets, step)], NEAR * step)
        for step in range(max(span for span, _ in sets))
    ]

    near, tight_done, tight_top, picked_queries, residual = call(
        functools.partial(local_kernel, rows, dim),
        [
            shape(each, NEAR, rows, LANES, dtype=jnp.float32),
            shape(each, NEAR, rows // 2, LANES, dtype=jnp.float32),
            shape(each, rows // 2, LANES, dtype=jnp.float32),
            shape(NEAR, rows // 2, LANES),
            shape(rows, cols),
        ],
        1,
        (index, chip, own_chip, selects, own_picked, own_tight, residual_in),
        3.4,
        [
            pltpu.VMEM((2, rows, LANES), bf16),
            pltpu.VMEM((each, 2, rows, LANES), bf16),
            pltpu.VMEM((each, NEAR, rows // 2, LANES), bf16),
            pltpu.VMEM((NEAR, rows // 2, LANES), bf16),
        ],
        vmem=12,
    )
    mixes = call(
        functools.partial(finish_kernel, sets, rows, dim),
        [shape(rows, LANES)] * NEAR,
        2,
        (head_offset, index, *far, picked_queries, near, tight_done, tight_top, selects, spreads),
        6.0,
        [
            pltpu.VMEM((each, NEAR, rows, LANES), jnp.float32),
            pltpu.VMEM((each, rows, LANES), jnp.float32),
            pltpu.VMEM((NEAR, rows, LANES), bf16),
        ],
        vmem=16,
    )
    mixes = [across(block, step) for step, block in enumerate(mixes)]
    other_mixes = [lax.ppermute(block, "tp", swap) for block in mixes]

    other_residual = lax.ppermute(residual, "tp", swap)
    width = norm_gain.shape[0]
    mine, theirs = [], []
    own = call(
        own_kernel,
        shape(rows, width, dtype=jnp.float32),
        1,
        (index, residual_in, other_residual, out_weight, *mixes),
        1.2,
        [pltpu.VMEM((rows, cols), bf16)],
    )
    step = rows // CHUNKS
    for number in range(CHUNKS):
        part = slice(number * step, (number + 1) * step)
        send, keep = call(
            functools.partial(block_kernel, part),
            [shape(step, cols), shape(step, cols, dtype=jnp.float32)],
            1,
            (
                index,
                own,
                *other_mixes,
                *other_weights,
                norm_gain.reshape(1, width),
                gate_weight,
                up_weight,
                down_weight,
            ),
            2.0,
            [
                pltpu.VMEM((step, width), jnp.float32),
                pltpu.VMEM((step, gate_weight.shape[1]), bf16),
                pltpu.VMEM((step, cols), bf16),
            ],
        )
        mine.append(keep)
        theirs.append(lax.ppermute(send, "tp", swap))
    return call(add_kernel, shape(rows, cols), 0, (*mine, *theirs), 0.8)


def solution(mesh):
    placed = (
        P("seq", "tp"),
        P("seq", "tp"),
        P("seq", "tp"),
        P("seq", "tp"),
        P(None, "tp"),
        P("tp", None),
        P(),
        P(None, "tp"),
        P(None, "tp"),
        P("tp", None),
    )
    return jax.shard_map(
        shards, mesh=mesh, in_specs=placed, out_specs=P("seq", "tp"), check_vma=False
    )
```

```python
import functools
import math

import jax
import jax.numpy as jnp
from jax import lax
from jax.experimental import pallas as pl
from jax.experimental.pallas import tpu as pltpu
from jax.sharding import PartitionSpec as P

BRANCHES = 6
LANES = 128
NEAR = 4
GROUP = LANES // NEAR
PEAK_FLOPS = 1153.5e12
MIB = 1024 * 1024
CHUNKS = 2

masked_score = -1e30


def part_rows(rows, branches):
    first, at = 0, {}
    for branch in branches:
        at[branch] = first
        first += rows // 2**branch
    return at, first


def far_sets(seq_count, rows):
    top_bits = min(seq_count.bit_length() - 1, BRANCHES)
    sets = {}
    for branch in range(2, BRANCHES):
        sets.setdefault(2 ** min(branch + 1, top_bits) // NEAR, []).append(branch)
    return sorted(sets.items())


def set_rows(sets, rows, each):
    first, at = 0, []
    for _, branches in sets:
        at.append(first)
        first += each * sum(rows // 2**branch for branch in branches)
    return at, first


def first_set(sets, step):
    return min(number for number, (span, _) in enumerate(sets) if span > step)


def even(count):
    return -(-count // 16) * 16


def mask_select(rows, branch, offset):
    rate = 2**branch
    count = rows // rate
    row = lax.broadcasted_iota(jnp.int32, (count, rows), 0)
    col = lax.broadcasted_iota(jnp.int32, (count, rows), 1)
    return jnp.where(col == row * rate + (offset & (rate - 1)), 1.0, 0.0)


def selection(rows, branches, offset_ref, head):
    select = [mask_select(rows, branch, offset_ref[branch, head]) for branch in branches]
    return jnp.concatenate(select, axis=0).astype(jnp.bfloat16)


def far_picks(sets, rows, dim, blocks, selects):
    each = LANES // dim
    far_branches = range(2, BRANCHES)
    starts, _ = part_rows(rows, far_branches)
    picked = []
    for (key, value), mine in zip(blocks, selects):
        for head in range(each):
            lanes = slice(head * dim, (head + 1) * dim)
            pairs = jnp.concatenate([key[:, lanes], value[:, lanes]], axis=1)
            picked.append(jnp.dot(mine[head], pairs, preferred_element_type=jnp.float32))
    outs = []
    for number in range(len(blocks)):
        parts = []
        for _, branches in sets:
            for branch in branches:
                first, last = starts[branch], starts[branch] + rows // 2**branch
                parts += [picked[number * each + head][first:last] for head in range(each)]
        outs.append(jnp.concatenate(parts, axis=0).astype(jnp.bfloat16))
    return outs


def split_kernel(sets, scale, dim, offset_ref, index_ref, source_ref, *out_refs):
    wide_refs, own_ref, core_ref, chip_ref = out_refs[:2], *out_refs[2:]
    rows = source_ref.shape[0] // 3
    low = index_ref[0] % NEAR
    all_lanes = [
        pl.ds(pl.multiple_of((low ^ side) * LANES, LANES), LANES) for side in range(NEAR)
    ]
    blocks = [
        (source_ref[rows : 2 * rows, lanes], source_ref[2 * rows :, lanes]) for lanes in all_lanes[2:]
    ]
    each = LANES // dim
    selects = [
        [selection(rows, range(2, BRANCHES), offset_ref, (low ^ side) * each + head) for head in range(each)]
        for side in (2, 3)
    ]
    picks = far_picks(sets, rows, dim, blocks, selects)
    for pick, wide_ref in zip(picks, wide_refs):
        wide_ref[...] = pick
    for side, lanes in enumerate(all_lanes):
        ref, first = ((own_ref, 0), (core_ref, 0), (chip_ref, 0), (core_ref, 3 * rows))[side]
        ref[first : first + rows] = source_ref[:rows, lanes] * jnp.asarray(scale, jnp.bfloat16)
        ref[first + rows : first + 3 * rows] = source_ref[rows:, lanes]


def turn_kernel(at, index_ref, *refs):
    in_refs, out_refs = refs[:NEAR], refs[NEAR + 1 : -1]
    low = index_ref[0] % NEAR
    for side in range(NEAR):
        for first, out_ref in zip(at, out_refs):
            out_ref[low ^ side] = in_refs[side][first:, :]


def attend(jobs, batch):
    dim = jobs[0][0].shape[1]
    lane = lax.broadcasted_iota(jnp.int32, (1, LANES), 1)
    keys = [pairs[:, :dim] for _, pairs, _, _ in jobs]
    values = [jnp.where(lane < dim, jnp.ones_like(pairs), pairs) for _, pairs, _, _ in jobs]
    pieces = []
    for number, (query, _, _, _) in enumerate(jobs):
        block = min(128, query.shape[0])
        pieces += [(start, number, block) for start in range(0, query.shape[0], block)]
    pieces.sort(key=lambda piece: piece[0])
    done = {}
    for at in range(0, len(pieces), batch):
        now = pieces[at : at + batch]
        scores = []
        for start, number, block in now:
            query, _, before, _ = jobs[number]
            scores.append(
                lax.dot_general(
                    query[start : start + block],
                    keys[number][: before + start + block],
                    (((1,), (1,)), ((), ())),
                    preferred_element_type=jnp.float32,
                )
            )
        masked = []
        for (start, number, block), score in zip(now, scores):
            _, _, before, columns = jobs[number]
            end = before + start + block
            if before == 0 and block == 128:
                row = lax.broadcasted_iota(jnp.int32, (block, block), 0)
                col = lax.broadcasted_iota(jnp.int32, (block, block), 1)
                last = jnp.where(col <= row, score[:, start:], masked_score)
                masked.append(jnp.concatenate([score[:, :start], last], axis=1) if start else last)
            else:
                row = lax.broadcasted_iota(jnp.int32, (block, end), 0)
                allowed = columns[:, :end] <= row + (before + start)
                masked.append(jnp.where(allowed, score, masked_score))
        tops = [jnp.max(score, axis=1, keepdims=True) for score in masked]
        weights = [jnp.exp(score - top).astype(jnp.bfloat16) for score, top in zip(masked, tops)]
        for piece, weight, top in zip(now, weights, tops):
            start, number, block = piece
            end = jobs[number][2] + start + block
            accum = jnp.dot(weight, values[number][:end], preferred_element_type=jnp.float32)
            done.setdefault(number, []).append((top, accum))
    return [
        tuple(jnp.concatenate(column, axis=0) for column in zip(*done[number]))
        for number in range(len(jobs))
    ]


def top_lanes(top, count, branch):
    length = top.shape[0]
    high = top.astype(jnp.bfloat16).astype(jnp.float32)
    middle = (top - high).astype(jnp.bfloat16).astype(jnp.float32)
    low = top - high - middle
    lane = lax.broadcasted_iota(jnp.int32, (length, LANES), 1)
    row = lax.broadcasted_iota(jnp.int32, (length, LANES), 0)
    lane = lane - ((row >> (count.bit_length() - 1)) * GROUP + 3 * branch)
    parts = jnp.where(lane == 0, high, jnp.where(lane == 1, middle, jnp.where(lane == 2, low, 0.0)))
    return jnp.sum(parts.reshape(NEAR, count, LANES), axis=0)


def nearest(members, rows, dim, low, query, pairs):
    each = LANES // dim
    for side, (query_in, key_in, value_in) in members:
        core = (low ^ side) % 2
        query[core] = query_in
        for head in range(each):
            lanes = slice(head * dim, (head + 1) * dim)
            pairs[head, core] = jnp.concatenate([key_in[:, lanes], value_in[:, lanes]], axis=1)
    return [
        (
            query[:, :, head * dim : (head + 1) * dim].reshape(2 * rows, dim),
            pairs[head].reshape(2 * rows, LANES),
            0,
            None,
        )
        for head in range(each)
    ]


def nearest_out(top, accum):
    lane = lax.broadcasted_iota(jnp.int32, (1, LANES), 1)
    return jnp.where(lane == 0, top, accum).reshape(2, top.shape[0] // 2, LANES)


def raw_blocks(ref, rows, first=0):
    return tuple(ref[first + part * rows : first + (part + 1) * rows] for part in range(3))


def local_picks(rows, dim, block, select_ref):
    query, key, value = block
    each = LANES // dim
    left = lax.broadcasted_iota(jnp.int32, (1, LANES), 1) < dim
    both = [jnp.dot(select_ref[head], query, preferred_element_type=jnp.float32) for head in range(each)]
    pairs = []
    for head in range(each):
        lanes = slice(head * dim, (head + 1) * dim)
        pair = jnp.concatenate([key[:, lanes], value[:, lanes]], axis=1)
        pair = jnp.dot(select_ref[head, : rows // 2], pair, preferred_element_type=jnp.float32)
        pairs.append(pair.astype(jnp.bfloat16))
    return jnp.where(left, both[0], both[1]).astype(jnp.bfloat16), pairs


def own_chip_kernel(sets, rows, dim, offset_ref, index_ref, own_ref, pair_ref, chip_ref, *refs):
    near_ref, pick_refs, relay_ref = refs[0], refs[1:3], refs[3]
    select_ref, spread_ref, picked_ref, tight_ref, query, pairs = refs[4:]
    half = chip_ref.shape[0]
    relay_ref[:half] = chip_ref[...]
    relay_ref[half:] = pair_ref[half:]
    each = LANES // dim
    low = index_ref[0] % NEAR
    starts, used = part_rows(rows, range(1, BRANCHES))
    column = lax.broadcasted_iota(jnp.int32, (1, rows), 1)
    row_wide = lax.broadcasted_iota(jnp.int32, (rows, rows), 0)
    for head in range(each):
        select = [mask_select(rows, b, offset_ref[b, low * each + head]) for b in range(1, BRANCHES)]
        select.append(jnp.zeros((rows - used, rows), jnp.float32))
        select_ref[head] = jnp.concatenate(select, axis=0).astype(jnp.bfloat16)
        target = jnp.full((1, rows), -1, jnp.int32)
        for branch in range(1, BRANCHES):
            rate = 2**branch
            offset = offset_ref[branch, low * each + head] & (rate - 1)
            target = jnp.where(
                column >= starts[branch], (column - starts[branch]) * rate + offset, target
            )
        spread_ref[head] = jnp.where(row_wide == target, 1.0, 0.0).astype(jnp.bfloat16)
    members = [(side, raw_blocks(ref, rows)) for side, ref in enumerate((own_ref, pair_ref))]
    selects = [select_ref[head, rows // 2 : used] for head in range(each)]
    blocks = [block[1:] for _, block in members]
    for pick, pick_ref in zip(far_picks(sets, rows, dim, blocks, [selects, selects]), pick_refs):
        pick_ref[...] = pick
    for side, block in members:
        picked, tight = local_picks(rows, dim, block, select_ref)
        core = (low ^ side) % 2
        picked_ref[core] = picked
        for head in range(each):
            tight_ref[head, core] = tight[head]
    jobs = nearest(members, rows, dim, low, query, pairs)
    for head, (top, accum) in enumerate(attend(jobs, 4)):
        near_ref[head] = nearest_out(top, accum)


def local_kernel(rows, dim, index_ref, *refs):
    chip_ref, own_chip_ref, select_ref, own_picked_ref, own_tight_ref, residual_ref = refs[:6]
    near_ref, far_ref, top_ref, picked_ref, residual_out = refs[6:11]
    query, pairs, tight_pairs, tight_query = refs[11:]
    residual_out[...] = residual_ref[...]
    each = LANES // dim
    low = index_ref[0] % NEAR
    chip = low // 2
    count = rows // 2
    blocks = {side: raw_blocks(chip_ref, rows, 3 * rows * (side - 2)) for side in (2, 3)}
    for core in range(2):
        tight_query[chip * 2 + core] = own_picked_ref[core, :count]
        picked_ref[chip * 2 + core] = own_picked_ref[core, count:]
        for head in range(each):
            tight_pairs[head, chip * 2 + core] = own_tight_ref[head, core]
    for side in (2, 3):
        picked, tight = local_picks(rows, dim, blocks[side], select_ref)
        tight_query[low ^ side] = picked[:count]
        picked_ref[low ^ side] = picked[count:]
        for head in range(each):
            tight_pairs[head, low ^ side] = tight[head]
    members = [(side, blocks[side]) for side in range(2, NEAR)]
    jobs = nearest(members, rows, dim, low, query, pairs)
    for head in range(each):
        near_ref[head, pl.ds(chip * 2, 2)] = own_chip_ref[head]
        jobs.append(
            (
                tight_query[:, :, head * dim : (head + 1) * dim].reshape(NEAR * count, dim),
                tight_pairs[head].reshape(NEAR * count, LANES),
                0,
                None,
            )
        )
    results = attend(jobs, 4)
    for head in range(each):
        near_ref[head, pl.ds((chip ^ 1) * 2, 2)] = nearest_out(*results[head])
        top, accum = results[each + head]
        far_ref[head] = accum.reshape(NEAR, count, LANES)
        top_ref[head] = top_lanes(top, count, 1)


def far_work(sets, rows, dim, index_ref, far_refs, query_ref, far, tops):
    each = LANES // dim
    group = index_ref[0] // NEAR
    starts, _ = part_rows(rows, range(1, BRANCHES))
    query_at, _ = part_rows(rows, range(2, BRANCHES))
    at, _ = set_rows(sets, rows, each)
    jobs, slots = [], []
    for number, (span, branches) in enumerate(sets):
        place = group % span
        first = at[number]
        for branch in branches:
            count = rows // 2**branch
            length = NEAR * count
            col = lax.broadcasted_iota(jnp.int32, (1, span * length), 1)
            step = span - 1 - (col >> (length.bit_length() - 1))
            columns = jnp.where((step == 0) | ((place ^ step) < place), col, 1 << 30)
            queries = query_ref[:, query_at[branch] : query_at[branch] + even(count), :]
            blocks = []
            for far_step in reversed(range(span)):
                skip = first - at[first_set(sets, far_step)]
                blocks.append(far_refs[far_step][:, skip : skip + each * count, :])
            if count % 16:
                queries = queries.astype(jnp.float32)[:, :count]
                blocks = [block.astype(jnp.float32) for block in blocks]
            for head in range(each):
                pairs = [block[:, head * count : (head + 1) * count].reshape(length, LANES) for block in blocks]
                pairs = jnp.concatenate(pairs, axis=0).astype(jnp.bfloat16)
                query = queries[:, :, head * dim : (head + 1) * dim].reshape(length, dim)
                jobs.append((query.astype(jnp.bfloat16), pairs, (span - 1) * length, columns))
                slots.append((branch, head, count))
            first += each * count
    for (branch, head, count), (top, accum) in zip(slots, attend(jobs, 2 * len(jobs))):
        into = slice(starts[branch], starts[branch] + count)
        far[head, :, into, :] = accum.reshape(NEAR, count, LANES)
        tops[head, into, :] = top_lanes(top, count, branch)


def hold_kernel(block_ref, ahead_ref, out_ref):
    out_ref[...] = block_ref[...]


def finish_kernel(sets, rows, dim, offset_ref, index_ref, *refs):
    steps = max(span for span, _ in sets)
    far_refs, refs = refs[:steps], refs[steps:]
    query_ref, near_ref, tight_ref, tight_top_ref, select_ref, spread_ref, refs = *refs[:6], refs[6:]
    out_refs, far, tops, mixed_ref = refs[:NEAR], *refs[NEAR:]
    each = LANES // dim
    low = index_ref[0] % NEAR
    starts, used = part_rows(rows, range(1, BRANCHES))
    tight = rows // 2
    for head in range(each):
        far[head, :, :tight, :] = tight_ref[head]
        far[head, :, used:, :] = jnp.zeros((NEAR, rows - used, LANES), jnp.float32)
        tops[head, :tight, :] = tight_top_ref[head]
        tops[head, used:, :] = jnp.zeros((rows - used, LANES), jnp.float32)
    far_work(sets, rows, dim, index_ref, far_refs, query_ref, far, tops)

    lane = lax.broadcasted_iota(jnp.int32, (1, LANES), 1)
    inside = lane % GROUP
    row = lax.broadcasted_iota(jnp.int32, (rows, 1), 0)
    row_lane = lax.broadcasted_iota(jnp.int32, (rows, LANES), 0)

    def along(start_of, value_of, fill):
        result = jnp.full(start_of.shape, fill, jnp.int32)
        for branch in range(1, BRANCHES):
            result = jnp.where(start_of >= starts[branch], value_of(branch), result)
        return result

    masks = jnp.zeros((1, LANES), jnp.int32)
    for branch in range(1, BRANCHES):
        masks = jnp.where(inside == 3 * branch, 2**branch - 1, masks)
    own_lane = along(row, lambda branch: 3 * branch, 0)

    def turned(array, lanes):
        return pltpu.roll(array, lanes % LANES, 1)

    heads = range(each)
    covered = []
    for head in heads:
        offsets = {
            branch: offset_ref[branch, low * each + head] & (2**branch - 1)
            for branch in range(1, BRANCHES)
        }
        chosen = jnp.where(inside == 0, 0, 1)
        for branch in range(1, BRANCHES):
            chosen = jnp.where(inside == 3 * branch, offsets[branch], chosen)
        covered.append((row_lane & masks) == chosen)
    stats = [
        jnp.dot(spread_ref[head], tops[head].astype(jnp.bfloat16), preferred_element_type=jnp.float32)
        for head in heads
    ]
    stats = [block + turned(block, -1) + turned(block, -2) for block in stats]
    for member in range(NEAR):
        stats = [
            jnp.where(lane == GROUP * member, near_ref[head, member][:, 0:1], stats[head]) for head in heads
        ]
    stats = [jnp.where(covered[head], stats[head], masked_score) for head in heads]
    peaks = stats
    for step in (3, 6, 12):
        peaks = [jnp.maximum(peak, turned(peak, -step)) for peak in peaks]
    peaks = [jnp.where(inside == 0, peak, masked_score) for peak in peaks]
    for step in (3, 6, 12):
        peaks = [jnp.maximum(peak, turned(peak, step)) for peak in peaks]
    weight = [
        jnp.where(block > 0.5 * masked_score, jnp.exp(block - peak), 0.0)
        for block, peak in zip(stats, peaks)
    ]
    weight = [block.astype(jnp.bfloat16) for block in weight]
    weights = [
        jnp.dot(select_ref[head], weight[head], preferred_element_type=jnp.float32) for head in heads
    ]
    from_lane = lax.broadcasted_iota(jnp.int32, (LANES, NEAR * LANES), 0)
    to_member = lax.broadcasted_iota(jnp.int32, (LANES, NEAR * LANES), 1) >> (LANES.bit_length() - 1)
    group = GROUP.bit_length() - 1
    any_lane = jnp.where(from_lane >> group == to_member, 1.0, 0.0).astype(jnp.bfloat16)
    first_lane = jnp.where(from_lane == to_member << group, 1.0, 0.0).astype(jnp.bfloat16)
    weights = [jnp.where(inside == own_lane, block, 0.0).astype(jnp.bfloat16) for block in weights]
    weights = [jnp.dot(block, any_lane, preferred_element_type=jnp.float32) for block in weights]
    owns = [jnp.dot(block, first_lane, preferred_element_type=jnp.float32) for block in weight]
    scaled = [[] for _ in heads]
    for member in range(NEAR):
        for head in heads:
            block = far[head, member] * weights[head][:, member * LANES : (member + 1) * LANES]
            rest = block - block.astype(jnp.bfloat16).astype(jnp.float32)
            scaled[head].append(jnp.where(lane == 0, rest, block).astype(jnp.bfloat16))
    added = [
        jnp.dot(spread_ref[head], jnp.concatenate(scaled[head], axis=1), preferred_element_type=jnp.float32)
        for head in heads
    ]
    halves = [[] for _ in heads]
    for member in range(NEAR):
        for head in heads:
            block = added[head][:, member * LANES : (member + 1) * LANES]
            own = owns[head][:, member * LANES : (member + 1) * LANES]
            total = block + own * near_ref[head, member]
            below = total[:, 1:2] + block[:, 0:1]
            halves[head].append(total[:, dim:] * (1.0 / below))
    for member in range(NEAR):
        pair = [mixed[member] for mixed in halves]
        mixed_ref[member] = jnp.concatenate(pair, axis=1).astype(jnp.bfloat16)
    for side in range(NEAR):
        out_refs[side][...] = mixed_ref[low ^ side]


def lay_out(low, block_refs, part, mix_ref):
    for side, ref in enumerate(block_refs):
        lanes = pl.ds(pl.multiple_of((low ^ side) * LANES, LANES), LANES)
        mix_ref[:, lanes] = ref[part, :]


def own_kernel(index_ref, residual_ref, other_residual_ref, weight_ref, *refs):
    block_refs, out_ref, mix_ref = refs[:NEAR], refs[NEAR], refs[NEAR + 1]
    rows, half = residual_ref.shape
    mine = pl.ds(pl.multiple_of(index_ref[1] * half, LANES), half)
    theirs = pl.ds(pl.multiple_of((1 - index_ref[1]) * half, LANES), half)
    lay_out(index_ref[0] % NEAR, block_refs, slice(0, rows), mix_ref)
    out_ref[...] = jnp.dot(mix_ref[...], weight_ref[...], preferred_element_type=jnp.float32)
    out_ref[:, mine] += residual_ref[...].astype(jnp.float32)
    out_ref[:, theirs] += other_residual_ref[...].astype(jnp.float32)


def block_kernel(part, index_ref, own_ref, *refs):
    block_refs, refs = refs[:NEAR], refs[NEAR:]
    first_weight_ref, second_weight_ref, gain_ref, gate_ref, up_ref, down_ref = refs[:6]
    theirs_ref, mine_ref, hidden_ref, act_ref, mix_ref = refs[6:]
    half = theirs_ref.shape[1]
    mine = pl.ds(pl.multiple_of(index_ref[1] * half, LANES), half)
    theirs = pl.ds(pl.multiple_of((1 - index_ref[1]) * half, LANES), half)
    count = first_weight_ref.shape[0]
    core = index_ref[0] % 2
    lay_out(index_ref[0] % NEAR, block_refs, part, mix_ref)
    hidden = own_ref[part, :]
    for place, weight_ref in ((core, first_weight_ref), (1 - core, second_weight_ref)):
        lanes = pl.ds(pl.multiple_of(place * count, LANES), count)
        hidden += jnp.dot(mix_ref[:, lanes], weight_ref[...], preferred_element_type=jnp.float32)
    hidden_ref[...] = hidden
    inverse = lax.rsqrt(jnp.mean(hidden * hidden, axis=1, keepdims=True) + 1e-05)
    normed = (hidden * inverse * gain_ref[...]).astype(jnp.bfloat16)
    step = 256
    for first in range(0, act_ref.shape[1], step):
        gate = jnp.dot(normed, gate_ref[:, first : first + step], preferred_element_type=jnp.float32)
        up = jnp.dot(normed, up_ref[:, first : first + step], preferred_element_type=jnp.float32)
        act_ref[:, first : first + step] = (gate / (1.0 + jnp.exp(-gate)) * up).astype(jnp.bfloat16)
    act = act_ref[...]
    theirs_ref[...] = jnp.dot(act, down_ref[:, theirs], preferred_element_type=jnp.float32).astype(
        jnp.bfloat16
    )
    mine_ref[...] = hidden_ref[:, mine] + jnp.dot(
        act, down_ref[:, mine], preferred_element_type=jnp.float32
    )


def add_kernel(*refs):
    count = (len(refs) - 1) // 2
    out_ref = refs[-1]
    for number in range(count):
        mine, theirs = refs[number], refs[count + number]
        step = mine.shape[0]
        out_ref[number * step : (number + 1) * step, :] = (
            mine[...] + theirs[...].astype(jnp.float32)
        ).astype(out_ref.dtype)


def call(kernel, out_shape, smem, operands, micros, scratch=(), vmem=8, passed=False):
    specs = [
        pl.BlockSpec(memory_space=pltpu.SMEM if number < smem else pltpu.VMEM)
        for number in range(len(operands))
    ]
    out_specs = jax.tree.map(lambda _: pl.BlockSpec(memory_space=pltpu.VMEM), out_shape)
    aliases = {}
    if passed:
        specs[-1] = out_specs[-1] = pl.BlockSpec(memory_space=pl.ANY)
        aliases = {len(specs) - 1: len(out_specs) - 1}
    return pl.pallas_call(
        kernel,
        out_shape=out_shape,
        in_specs=specs,
        out_specs=out_specs,
        input_output_aliases=aliases,
        scratch_shapes=list(scratch),
        compiler_params=pltpu.CompilerParams(vmem_limit_bytes=vmem * MIB),
        cost_estimate=pl.CostEstimate(
            flops=int(micros * PEAK_FLOPS / 1e6), bytes_accessed=0, transcendentals=0
        ),
    )(*operands)


def shards(
    residual_in,
    queries,
    keys,
    values,
    head_offset,
    out_weight,
    norm_gain,
    gate_weight,
    up_weight,
    down_weight,
):
    rows, cols = queries.shape
    heads = head_offset.shape[1]
    dim = cols // heads
    each = heads // NEAR
    seq_count = lax.axis_size("seq")
    scale = 1.0 / math.sqrt(dim)
    sets = far_sets(seq_count, rows)
    index = jnp.stack([lax.axis_index("seq"), lax.axis_index("tp")]).astype(jnp.int32)
    bf16 = jnp.bfloat16

    def shape(*sizes, dtype=bf16):
        return jax.ShapeDtypeStruct(sizes, dtype)

    def across(block, distance):
        if distance == 0:
            return block
        return lax.ppermute(block, "seq", [(i, i ^ distance) for i in range(seq_count)])

    swap = [(0, 1), (1, 0)]
    half = out_weight.shape[0] // 2
    part = lax.dynamic_slice_in_dim(out_weight, lax.axis_index("seq") % 2 * half, half)
    part = lax.ppermute(part, "tp", swap)
    other_weights = (part, across(part, 1))

    source = jnp.concatenate([queries, keys, values], axis=0)
    _, tall = part_rows(rows, range(2, BRANCHES))
    first, second, own, core, chip = call(
        functools.partial(split_kernel, sets, scale, dim),
        [shape(each * tall, LANES)] * 2 + [shape(part * rows, LANES) for part in (3, 6, 3)],
        2,
        (head_offset, index, source),
        1.0,
        vmem=12,
    )
    wide = [across(first, 2), across(second, 3)]
    core = across(core, 1)
    own_chip, first, second, relay, selects, spreads, own_picked, own_tight = call(
        functools.partial(own_chip_kernel, sets, rows, dim),
        [shape(each, 2, rows, LANES, dtype=jnp.float32)] + [shape(each * tall, LANES)] * 2
        + [shape(6 * rows, LANES)]
        + [shape(each, rows, rows)] * 2
        + [shape(2, rows, LANES), shape(each, 2, rows // 2, LANES)],
        2,
        (head_offset, index, own, core, chip),
        2.4,
        [pltpu.VMEM((2, rows, LANES), bf16), pltpu.VMEM((each, 2, rows, LANES), bf16)],
        vmem=12,
    )
    at, all_rows = set_rows(sets, rows, each)
    *turned, relay = call(
        functools.partial(turn_kernel, at),
        [shape(NEAR, all_rows - first, LANES) for first in at] + [shape(6 * rows, LANES)],
        1,
        (index, first, second, *wide, relay),
        0.3,
        passed=True,
    )
    chip = across(relay, 2)
    far = [
        across(turned[first_set(sets, step)], NEAR * step)
        for step in range(max(span for span, _ in sets))
    ]

    near, tight_done, tight_top, picked_queries, residual = call(
        functools.partial(local_kernel, rows, dim),
        [
            shape(each, NEAR, rows, LANES, dtype=jnp.float32),
            shape(each, NEAR, rows // 2, LANES, dtype=jnp.float32),
            shape(each, rows // 2, LANES, dtype=jnp.float32),
            shape(NEAR, rows // 2, LANES),
            shape(rows, cols),
        ],
        1,
        (index, chip, own_chip, selects, own_picked, own_tight, residual_in),
        3.4,
        [
            pltpu.VMEM((2, rows, LANES), bf16),
            pltpu.VMEM((each, 2, rows, LANES), bf16),
            pltpu.VMEM((each, NEAR, rows // 2, LANES), bf16),
            pltpu.VMEM((NEAR, rows // 2, LANES), bf16),
        ],
        vmem=12,
    )
    mixes = call(
        functools.partial(finish_kernel, sets, rows, dim),
        [shape(rows, LANES)] * NEAR,
        2,
        (head_offset, index, *far, picked_queries, near, tight_done, tight_top, selects, spreads),
        6.0,
        [
            pltpu.VMEM((each, NEAR, rows, LANES), jnp.float32),
            pltpu.VMEM((each, rows, LANES), jnp.float32),
            pltpu.VMEM((NEAR, rows, LANES), bf16),
        ],
        vmem=16,
    )
    mixes = [mixes[0], across(mixes[1], 1), across(mixes[2], 2), mixes[3]]
    held = call(hold_kernel, shape(rows, LANES), 0, (mixes[3], mixes[1]), 0.2)
    mixes[3] = across(held, 3)
    other_mixes = [lax.ppermute(block, "tp", swap) for block in mixes]

    other_residual = lax.ppermute(residual, "tp", swap)
    width = norm_gain.shape[0]
    mine, theirs = [], []
    own = call(
        own_kernel,
        shape(rows, width, dtype=jnp.float32),
        1,
        (index, residual_in, other_residual, out_weight, *mixes),
        1.2,
        [pltpu.VMEM((rows, cols), bf16)],
    )
    step = rows // CHUNKS
    for number in range(CHUNKS):
        part = slice(number * step, (number + 1) * step)
        send, keep = call(
            functools.partial(block_kernel, part),
            [shape(step, cols), shape(step, cols, dtype=jnp.float32)],
            1,
            (
                index,
                own,
                *other_mixes,
                *other_weights,
                norm_gain.reshape(1, width),
                gate_weight,
                up_weight,
                down_weight,
            ),
            2.0,
            [
                pltpu.VMEM((step, width), jnp.float32),
                pltpu.VMEM((step, gate_weight.shape[1]), bf16),
                pltpu.VMEM((step, cols), bf16),
            ],
        )
        mine.append(keep)
        theirs.append(lax.ppermute(send, "tp", swap))
    return call(add_kernel, shape(rows, cols), 0, (*mine, *theirs), 0.8)


def solution(mesh):
    placed = (
        P("seq", "tp"),
        P("seq", "tp"),
        P("seq", "tp"),
        P("seq", "tp"),
        P(None, "tp"),
        P("tp", None),
        P(),
        P(None, "tp"),
        P(None, "tp"),
        P("tp", None),
    )
    return jax.shard_map(
        shards, mesh=mesh, in_specs=placed, out_specs=P("seq", "tp"), check_vma=False
    )
```

```python
import functools
import math

import jax
import jax.numpy as jnp
from jax import lax
from jax.experimental import pallas as pl
from jax.experimental.pallas import tpu as pltpu
from jax.sharding import PartitionSpec as P

BRANCHES = 6
LANES = 128
NEAR = 4
GROUP = LANES // NEAR
PEAK_FLOPS = 1153.5e12
MIB = 1024 * 1024
CHUNKS = 2

masked_score = -1e30


def part_rows(rows, branches):
    first, at = 0, {}
    for branch in branches:
        at[branch] = first
        first += rows // 2**branch
    return at, first


def far_sets(seq_count, rows):
    top_bits = min(seq_count.bit_length() - 1, BRANCHES)
    sets = {}
    for branch in range(2, BRANCHES):
        sets.setdefault(2 ** min(branch + 1, top_bits) // NEAR, []).append(branch)
    return sorted(sets.items())


def set_rows(sets, rows, each):
    first, at = 0, []
    for _, branches in sets:
        at.append(first)
        first += each * sum(rows // 2**branch for branch in branches)
    return at, first


def first_set(sets, step):
    return min(number for number, (span, _) in enumerate(sets) if span > step)


def even(count):
    return -(-count // 16) * 16


def mask_select(rows, branch, offset):
    rate = 2**branch
    count = rows // rate
    row = lax.broadcasted_iota(jnp.int32, (count, rows), 0)
    col = lax.broadcasted_iota(jnp.int32, (count, rows), 1)
    return jnp.where(col == row * rate + (offset & (rate - 1)), 1.0, 0.0)


def selection(rows, branches, offset_ref, head):
    select = [mask_select(rows, branch, offset_ref[branch, head]) for branch in branches]
    return jnp.concatenate(select, axis=0).astype(jnp.bfloat16)


def far_picks(sets, rows, dim, blocks, selects):
    each = LANES // dim
    far_branches = range(2, BRANCHES)
    starts, _ = part_rows(rows, far_branches)
    picked = []
    for (key, value), mine in zip(blocks, selects):
        for head in range(each):
            lanes = slice(head * dim, (head + 1) * dim)
            pairs = jnp.concatenate([key[:, lanes], value[:, lanes]], axis=1)
            picked.append(jnp.dot(mine[head], pairs, preferred_element_type=jnp.float32))
    outs = []
    for number in range(len(blocks)):
        parts = []
        for _, branches in sets:
            for branch in branches:
                first, last = starts[branch], starts[branch] + rows // 2**branch
                parts += [picked[number * each + head][first:last] for head in range(each)]
        outs.append(jnp.concatenate(parts, axis=0).astype(jnp.bfloat16))
    return outs


def split_kernel(sets, scale, dim, offset_ref, index_ref, source_ref, *out_refs):
    wide_refs, own_ref, core_ref, chip_ref = out_refs[:2], *out_refs[2:]
    rows = source_ref.shape[0] // 3
    low = index_ref[0] % NEAR
    all_lanes = [
        pl.ds(pl.multiple_of((low ^ side) * LANES, LANES), LANES) for side in range(NEAR)
    ]
    blocks = [
        (source_ref[rows : 2 * rows, lanes], source_ref[2 * rows :, lanes]) for lanes in all_lanes[2:]
    ]
    each = LANES // dim
    selects = [
        [selection(rows, range(2, BRANCHES), offset_ref, (low ^ side) * each + head) for head in range(each)]
        for side in (2, 3)
    ]
    picks = far_picks(sets, rows, dim, blocks, selects)
    for pick, wide_ref in zip(picks, wide_refs):
        wide_ref[...] = pick
    for side, lanes in enumerate(all_lanes):
        ref, first = ((own_ref, 0), (core_ref, 0), (chip_ref, 0), (core_ref, 3 * rows))[side]
        ref[first : first + rows] = source_ref[:rows, lanes] * jnp.asarray(scale, jnp.bfloat16)
        ref[first + rows : first + 3 * rows] = source_ref[rows:, lanes]


def turn_kernel(at, index_ref, *refs):
    in_refs, out_refs = refs[:NEAR], refs[NEAR + 1 : -1]
    low = index_ref[0] % NEAR
    for side in range(NEAR):
        for first, out_ref in zip(at, out_refs):
            out_ref[low ^ side] = in_refs[side][first:, :]


def attend(jobs, batch):
    dim = jobs[0][0].shape[1]
    lane = lax.broadcasted_iota(jnp.int32, (1, LANES), 1)
    keys = [pairs[:, :dim] for _, pairs, _, _ in jobs]
    values = [jnp.where(lane < dim, jnp.ones_like(pairs), pairs) for _, pairs, _, _ in jobs]
    pieces = []
    for number, (query, _, _, _) in enumerate(jobs):
        block = min(128, query.shape[0])
        pieces += [(start, number, block) for start in range(0, query.shape[0], block)]
    pieces.sort(key=lambda piece: piece[0])
    done = {}
    for at in range(0, len(pieces), batch):
        now = pieces[at : at + batch]
        scores = []
        for start, number, block in now:
            query, _, before, _ = jobs[number]
            scores.append(
                lax.dot_general(
                    query[start : start + block],
                    keys[number][: before + start + block],
                    (((1,), (1,)), ((), ())),
                    preferred_element_type=jnp.float32,
                )
            )
        masked = []
        for (start, number, block), score in zip(now, scores):
            _, _, before, columns = jobs[number]
            end = before + start + block
            if before == 0 and block == 128:
                row = lax.broadcasted_iota(jnp.int32, (block, block), 0)
                col = lax.broadcasted_iota(jnp.int32, (block, block), 1)
                last = jnp.where(col <= row, score[:, start:], masked_score)
                masked.append(jnp.concatenate([score[:, :start], last], axis=1) if start else last)
            else:
                row = lax.broadcasted_iota(jnp.int32, (block, end), 0)
                allowed = columns[:, :end] <= row + (before + start)
                masked.append(jnp.where(allowed, score, masked_score))
        tops = [jnp.max(score, axis=1, keepdims=True) for score in masked]
        weights = [jnp.exp(score - top).astype(jnp.bfloat16) for score, top in zip(masked, tops)]
        for piece, weight, top in zip(now, weights, tops):
            start, number, block = piece
            end = jobs[number][2] + start + block
            accum = jnp.dot(weight, values[number][:end], preferred_element_type=jnp.float32)
            done.setdefault(number, []).append((top, accum))
    return [
        tuple(jnp.concatenate(column, axis=0) for column in zip(*done[number]))
        for number in range(len(jobs))
    ]


def top_lanes(top, count, branch):
    length = top.shape[0]
    high = top.astype(jnp.bfloat16).astype(jnp.float32)
    middle = (top - high).astype(jnp.bfloat16).astype(jnp.float32)
    low = top - high - middle
    lane = lax.broadcasted_iota(jnp.int32, (length, LANES), 1)
    row = lax.broadcasted_iota(jnp.int32, (length, LANES), 0)
    lane = lane - ((row >> (count.bit_length() - 1)) * GROUP + 3 * branch)
    parts = jnp.where(lane == 0, high, jnp.where(lane == 1, middle, jnp.where(lane == 2, low, 0.0)))
    return jnp.sum(parts.reshape(NEAR, count, LANES), axis=0)


def nearest(members, rows, dim, low, query, pairs):
    each = LANES // dim
    for side, (query_in, key_in, value_in) in members:
        core = (low ^ side) % 2
        query[core] = query_in
        for head in range(each):
            lanes = slice(head * dim, (head + 1) * dim)
            pairs[head, core] = jnp.concatenate([key_in[:, lanes], value_in[:, lanes]], axis=1)
    return [
        (
            query[:, :, head * dim : (head + 1) * dim].reshape(2 * rows, dim),
            pairs[head].reshape(2 * rows, LANES),
            0,
            None,
        )
        for head in range(each)
    ]


def nearest_out(top, accum):
    lane = lax.broadcasted_iota(jnp.int32, (1, LANES), 1)
    return jnp.where(lane == 0, top, accum).reshape(2, top.shape[0] // 2, LANES)


def raw_blocks(ref, rows, first=0):
    return tuple(ref[first + part * rows : first + (part + 1) * rows] for part in range(3))


def local_picks(rows, dim, block, select_ref):
    query, key, value = block
    each = LANES // dim
    left = lax.broadcasted_iota(jnp.int32, (1, LANES), 1) < dim
    both = [jnp.dot(select_ref[head], query, preferred_element_type=jnp.float32) for head in range(each)]
    pairs = []
    for head in range(each):
        lanes = slice(head * dim, (head + 1) * dim)
        pair = jnp.concatenate([key[:, lanes], value[:, lanes]], axis=1)
        pair = jnp.dot(select_ref[head, : rows // 2], pair, preferred_element_type=jnp.float32)
        pairs.append(pair.astype(jnp.bfloat16))
    return jnp.where(left, both[0], both[1]).astype(jnp.bfloat16), pairs


def own_chip_kernel(sets, rows, dim, offset_ref, index_ref, own_ref, pair_ref, chip_ref, *refs):
    near_ref, pick_refs, relay_ref = refs[0], refs[1:3], refs[3]
    select_ref, spread_ref, picked_ref, tight_ref, query, pairs = refs[4:]
    half = chip_ref.shape[0]
    relay_ref[:half] = chip_ref[...]
    relay_ref[half:] = pair_ref[half:]
    each = LANES // dim
    low = index_ref[0] % NEAR
    starts, used = part_rows(rows, range(1, BRANCHES))
    column = lax.broadcasted_iota(jnp.int32, (1, rows), 1)
    row_wide = lax.broadcasted_iota(jnp.int32, (rows, rows), 0)
    for head in range(each):
        select = [mask_select(rows, b, offset_ref[b, low * each + head]) for b in range(1, BRANCHES)]
        select.append(jnp.zeros((rows - used, rows), jnp.float32))
        select_ref[head] = jnp.concatenate(select, axis=0).astype(jnp.bfloat16)
        target = jnp.full((1, rows), -1, jnp.int32)
        for branch in range(1, BRANCHES):
            rate = 2**branch
            offset = offset_ref[branch, low * each + head] & (rate - 1)
            target = jnp.where(
                column >= starts[branch], (column - starts[branch]) * rate + offset, target
            )
        spread_ref[head] = jnp.where(row_wide == target, 1.0, 0.0).astype(jnp.bfloat16)
    members = [(side, raw_blocks(ref, rows)) for side, ref in enumerate((own_ref, pair_ref))]
    selects = [select_ref[head, rows // 2 : used] for head in range(each)]
    blocks = [block[1:] for _, block in members]
    for pick, pick_ref in zip(far_picks(sets, rows, dim, blocks, [selects, selects]), pick_refs):
        pick_ref[...] = pick
    for side, block in members:
        picked, tight = local_picks(rows, dim, block, select_ref)
        core = (low ^ side) % 2
        picked_ref[core] = picked
        for head in range(each):
            tight_ref[head, core] = tight[head]
    jobs = nearest(members, rows, dim, low, query, pairs)
    for head, (top, accum) in enumerate(attend(jobs, 4)):
        near_ref[head] = nearest_out(top, accum)


def local_kernel(rows, dim, index_ref, *refs):
    chip_ref, own_chip_ref, select_ref, own_picked_ref, own_tight_ref, residual_ref = refs[:6]
    near_ref, far_ref, top_ref, picked_ref, residual_out = refs[6:11]
    query, pairs, tight_pairs, tight_query = refs[11:]
    residual_out[...] = residual_ref[...]
    each = LANES // dim
    low = index_ref[0] % NEAR
    chip = low // 2
    count = rows // 2
    blocks = {side: raw_blocks(chip_ref, rows, 3 * rows * (side - 2)) for side in (2, 3)}
    for core in range(2):
        tight_query[chip * 2 + core] = own_picked_ref[core, :count]
        picked_ref[chip * 2 + core] = own_picked_ref[core, count:]
        for head in range(each):
            tight_pairs[head, chip * 2 + core] = own_tight_ref[head, core]
    for side in (2, 3):
        picked, tight = local_picks(rows, dim, blocks[side], select_ref)
        tight_query[low ^ side] = picked[:count]
        picked_ref[low ^ side] = picked[count:]
        for head in range(each):
            tight_pairs[head, low ^ side] = tight[head]
    members = [(side, blocks[side]) for side in range(2, NEAR)]
    jobs = nearest(members, rows, dim, low, query, pairs)
    for head in range(each):
        near_ref[head, pl.ds(chip * 2, 2)] = own_chip_ref[head]
        jobs.append(
            (
                tight_query[:, :, head * dim : (head + 1) * dim].reshape(NEAR * count, dim),
                tight_pairs[head].reshape(NEAR * count, LANES),
                0,
                None,
            )
        )
    results = attend(jobs, 4)
    for head in range(each):
        near_ref[head, pl.ds((chip ^ 1) * 2, 2)] = nearest_out(*results[head])
        top, accum = results[each + head]
        far_ref[head] = accum.reshape(NEAR, count, LANES)
        top_ref[head] = top_lanes(top, count, 1)


def far_work(sets, rows, dim, index_ref, far_refs, query_ref, far, tops):
    each = LANES // dim
    group = index_ref[0] // NEAR
    starts, _ = part_rows(rows, range(1, BRANCHES))
    query_at, _ = part_rows(rows, range(2, BRANCHES))
    at, _ = set_rows(sets, rows, each)
    jobs, slots = [], []
    for number, (span, branches) in enumerate(sets):
        place = group % span
        first = at[number]
        for branch in branches:
            count = rows // 2**branch
            length = NEAR * count
            col = lax.broadcasted_iota(jnp.int32, (1, span * length), 1)
            step = span - 1 - (col >> (length.bit_length() - 1))
            columns = jnp.where((step == 0) | ((place ^ step) < place), col, 1 << 30)
            queries = query_ref[:, query_at[branch] : query_at[branch] + even(count), :]
            blocks = []
            for far_step in reversed(range(span)):
                skip = first - at[first_set(sets, far_step)]
                blocks.append(far_refs[far_step][:, skip : skip + each * count, :])
            if count % 16:
                queries = queries.astype(jnp.float32)[:, :count]
                blocks = [block.astype(jnp.float32) for block in blocks]
            for head in range(each):
                pairs = [block[:, head * count : (head + 1) * count].reshape(length, LANES) for block in blocks]
                pairs = jnp.concatenate(pairs, axis=0).astype(jnp.bfloat16)
                query = queries[:, :, head * dim : (head + 1) * dim].reshape(length, dim)
                jobs.append((query.astype(jnp.bfloat16), pairs, (span - 1) * length, columns))
                slots.append((branch, head, count))
            first += each * count
    for (branch, head, count), (top, accum) in zip(slots, attend(jobs, 2 * len(jobs))):
        into = slice(starts[branch], starts[branch] + count)
        far[head, :, into, :] = accum.reshape(NEAR, count, LANES)
        tops[head, into, :] = top_lanes(top, count, branch)


def hold_kernel(block_ref, own_ref, core_ref, out_ref, both_ref):
    out_ref[...] = block_ref[...]
    rows = own_ref.shape[0]
    both_ref[:rows] = own_ref[...]
    both_ref[rows:] = core_ref[...]


def finish_kernel(sets, rows, dim, offset_ref, index_ref, *refs):
    steps = max(span for span, _ in sets)
    far_refs, refs = refs[:steps], refs[steps:]
    query_ref, near_ref, tight_ref, tight_top_ref, select_ref, spread_ref, refs = *refs[:6], refs[6:]
    out_refs, far, tops, mixed_ref = refs[:NEAR], *refs[NEAR:]
    each = LANES // dim
    low = index_ref[0] % NEAR
    starts, used = part_rows(rows, range(1, BRANCHES))
    tight = rows // 2
    for head in range(each):
        far[head, :, :tight, :] = tight_ref[head]
        far[head, :, used:, :] = jnp.zeros((NEAR, rows - used, LANES), jnp.float32)
        tops[head, :tight, :] = tight_top_ref[head]
        tops[head, used:, :] = jnp.zeros((rows - used, LANES), jnp.float32)
    far_work(sets, rows, dim, index_ref, far_refs, query_ref, far, tops)

    lane = lax.broadcasted_iota(jnp.int32, (1, LANES), 1)
    inside = lane % GROUP
    row = lax.broadcasted_iota(jnp.int32, (rows, 1), 0)
    row_lane = lax.broadcasted_iota(jnp.int32, (rows, LANES), 0)

    def along(start_of, value_of, fill):
        result = jnp.full(start_of.shape, fill, jnp.int32)
        for branch in range(1, BRANCHES):
            result = jnp.where(start_of >= starts[branch], value_of(branch), result)
        return result

    masks = jnp.zeros((1, LANES), jnp.int32)
    for branch in range(1, BRANCHES):
        masks = jnp.where(inside == 3 * branch, 2**branch - 1, masks)
    own_lane = along(row, lambda branch: 3 * branch, 0)

    def turned(array, lanes):
        return pltpu.roll(array, lanes % LANES, 1)

    heads = range(each)
    covered = []
    for head in heads:
        offsets = {
            branch: offset_ref[branch, low * each + head] & (2**branch - 1)
            for branch in range(1, BRANCHES)
        }
        chosen = jnp.where(inside == 0, 0, 1)
        for branch in range(1, BRANCHES):
            chosen = jnp.where(inside == 3 * branch, offsets[branch], chosen)
        covered.append((row_lane & masks) == chosen)
    stats = [
        jnp.dot(spread_ref[head], tops[head].astype(jnp.bfloat16), preferred_element_type=jnp.float32)
        for head in heads
    ]
    stats = [block + turned(block, -1) + turned(block, -2) for block in stats]
    for member in range(NEAR):
        stats = [
            jnp.where(lane == GROUP * member, near_ref[head, member][:, 0:1], stats[head]) for head in heads
        ]
    stats = [jnp.where(covered[head], stats[head], masked_score) for head in heads]
    peaks = stats
    for step in (3, 6, 12):
        peaks = [jnp.maximum(peak, turned(peak, -step)) for peak in peaks]
    peaks = [jnp.where(inside == 0, peak, masked_score) for peak in peaks]
    for step in (3, 6, 12):
        peaks = [jnp.maximum(peak, turned(peak, step)) for peak in peaks]
    weight = [
        jnp.where(block > 0.5 * masked_score, jnp.exp(block - peak), 0.0)
        for block, peak in zip(stats, peaks)
    ]
    weight = [block.astype(jnp.bfloat16) for block in weight]
    weights = [
        jnp.dot(select_ref[head], weight[head], preferred_element_type=jnp.float32) for head in heads
    ]
    from_lane = lax.broadcasted_iota(jnp.int32, (LANES, NEAR * LANES), 0)
    to_member = lax.broadcasted_iota(jnp.int32, (LANES, NEAR * LANES), 1) >> (LANES.bit_length() - 1)
    group = GROUP.bit_length() - 1
    any_lane = jnp.where(from_lane >> group == to_member, 1.0, 0.0).astype(jnp.bfloat16)
    first_lane = jnp.where(from_lane == to_member << group, 1.0, 0.0).astype(jnp.bfloat16)
    weights = [jnp.where(inside == own_lane, block, 0.0).astype(jnp.bfloat16) for block in weights]
    weights = [jnp.dot(block, any_lane, preferred_element_type=jnp.float32) for block in weights]
    owns = [jnp.dot(block, first_lane, preferred_element_type=jnp.float32) for block in weight]
    scaled = [[] for _ in heads]
    for member in range(NEAR):
        for head in heads:
            block = far[head, member] * weights[head][:, member * LANES : (member + 1) * LANES]
            rest = block - block.astype(jnp.bfloat16).astype(jnp.float32)
            scaled[head].append(jnp.where(lane == 0, rest, block).astype(jnp.bfloat16))
    added = [
        jnp.dot(spread_ref[head], jnp.concatenate(scaled[head], axis=1), preferred_element_type=jnp.float32)
        for head in heads
    ]
    halves = [[] for _ in heads]
    for member in range(NEAR):
        for head in heads:
            block = added[head][:, member * LANES : (member + 1) * LANES]
            own = owns[head][:, member * LANES : (member + 1) * LANES]
            total = block + own * near_ref[head, member]
            below = total[:, 1:2] + block[:, 0:1]
            halves[head].append(total[:, dim:] * (1.0 / below))
    for member in range(NEAR):
        pair = [mixed[member] for mixed in halves]
        mixed_ref[member] = jnp.concatenate(pair, axis=1).astype(jnp.bfloat16)
    for side in range(NEAR):
        out_refs[side][...] = mixed_ref[low ^ side]


def lay_out(low, block_refs, part, mix_ref):
    for side, ref in enumerate(block_refs):
        lanes = pl.ds(pl.multiple_of((low ^ side) * LANES, LANES), LANES)
        mix_ref[:, lanes] = ref[part, :]


def halve_kernel(first_ref, second_ref, *out_refs):
    step = out_refs[0].shape[0] // 2
    for number, out_ref in enumerate(out_refs):
        part = slice(number * step, (number + 1) * step)
        out_ref[:step] = first_ref[part, :]
        out_ref[step:] = second_ref[part, :]


def own_kernel(index_ref, residual_ref, other_residual_ref, weight_ref, *refs):
    block_refs, out_ref, mix_ref = refs[:NEAR], refs[NEAR], refs[NEAR + 1]
    rows, half = residual_ref.shape
    mine = pl.ds(pl.multiple_of(index_ref[1] * half, LANES), half)
    theirs = pl.ds(pl.multiple_of((1 - index_ref[1]) * half, LANES), half)
    lay_out(index_ref[0] % NEAR, block_refs, slice(0, rows), mix_ref)
    out_ref[...] = jnp.dot(mix_ref[...], weight_ref[...], preferred_element_type=jnp.float32)
    out_ref[:, mine] += residual_ref[...].astype(jnp.float32)
    out_ref[:, theirs] += other_residual_ref[...].astype(jnp.float32)


def block_kernel(part, places, index_ref, own_ref, *refs):
    block_refs, refs = refs[:2], refs[2:]
    first_weight_ref, second_weight_ref, gain_ref, gate_ref, up_ref, down_ref = refs[:6]
    theirs_ref, mine_ref, hidden_ref, act_ref, mix_ref = refs[6:]
    half = theirs_ref.shape[1]
    mine = pl.ds(pl.multiple_of(index_ref[1] * half, LANES), half)
    theirs = pl.ds(pl.multiple_of((1 - index_ref[1]) * half, LANES), half)
    count = first_weight_ref.shape[0]
    core = index_ref[0] % 2
    rows = mix_ref.shape[0]
    for side, (place, first) in enumerate(places):
        lanes = pl.ds(pl.multiple_of((index_ref[0] % NEAR ^ side) * LANES, LANES), LANES)
        mix_ref[:, lanes] = block_refs[place][first : first + rows, :]
    hidden = own_ref[part, :]
    for place, weight_ref in ((core, first_weight_ref), (1 - core, second_weight_ref)):
        lanes = pl.ds(pl.multiple_of(place * count, LANES), count)
        hidden += jnp.dot(mix_ref[:, lanes], weight_ref[...], preferred_element_type=jnp.float32)
    hidden_ref[...] = hidden
    inverse = lax.rsqrt(jnp.mean(hidden * hidden, axis=1, keepdims=True) + 1e-05)
    normed = (hidden * inverse * gain_ref[...]).astype(jnp.bfloat16)
    step = 256
    for first in range(0, act_ref.shape[1], step):
        gate = jnp.dot(normed, gate_ref[:, first : first + step], preferred_element_type=jnp.float32)
        up = jnp.dot(normed, up_ref[:, first : first + step], preferred_element_type=jnp.float32)
        act_ref[:, first : first + step] = (gate / (1.0 + jnp.exp(-gate)) * up).astype(jnp.bfloat16)
    act = act_ref[...]
    theirs_ref[...] = jnp.dot(act, down_ref[:, theirs], preferred_element_type=jnp.float32).astype(
        jnp.bfloat16
    )
    mine_ref[...] = hidden_ref[:, mine] + jnp.dot(
        act, down_ref[:, mine], preferred_element_type=jnp.float32
    )


def add_kernel(*refs):
    count = (len(refs) - 1) // 2
    out_ref = refs[-1]
    for number in range(count):
        mine, theirs = refs[number], refs[count + number]
        step = mine.shape[0]
        out_ref[number * step : (number + 1) * step, :] = (
            mine[...] + theirs[...].astype(jnp.float32)
        ).astype(out_ref.dtype)


def call(kernel, out_shape, smem, operands, micros, scratch=(), vmem=8, passed=False):
    specs = [
        pl.BlockSpec(memory_space=pltpu.SMEM if number < smem else pltpu.VMEM)
        for number in range(len(operands))
    ]
    out_specs = jax.tree.map(lambda _: pl.BlockSpec(memory_space=pltpu.VMEM), out_shape)
    aliases = {}
    if passed:
        specs[-1] = out_specs[-1] = pl.BlockSpec(memory_space=pl.ANY)
        aliases = {len(specs) - 1: len(out_specs) - 1}
    return pl.pallas_call(
        kernel,
        out_shape=out_shape,
        in_specs=specs,
        out_specs=out_specs,
        input_output_aliases=aliases,
        scratch_shapes=list(scratch),
        compiler_params=pltpu.CompilerParams(vmem_limit_bytes=vmem * MIB),
        cost_estimate=pl.CostEstimate(
            flops=int(micros * PEAK_FLOPS / 1e6), bytes_accessed=0, transcendentals=0
        ),
    )(*operands)


def shards(
    residual_in,
    queries,
    keys,
    values,
    head_offset,
    out_weight,
    norm_gain,
    gate_weight,
    up_weight,
    down_weight,
):
    rows, cols = queries.shape
    heads = head_offset.shape[1]
    dim = cols // heads
    each = heads // NEAR
    seq_count = lax.axis_size("seq")
    scale = 1.0 / math.sqrt(dim)
    sets = far_sets(seq_count, rows)
    index = jnp.stack([lax.axis_index("seq"), lax.axis_index("tp")]).astype(jnp.int32)
    bf16 = jnp.bfloat16

    def shape(*sizes, dtype=bf16):
        return jax.ShapeDtypeStruct(sizes, dtype)

    def across(block, distance):
        if distance == 0:
            return block
        return lax.ppermute(block, "seq", [(i, i ^ distance) for i in range(seq_count)])

    swap = [(0, 1), (1, 0)]
    half = out_weight.shape[0] // 2
    part = lax.dynamic_slice_in_dim(out_weight, lax.axis_index("seq") % 2 * half, half)
    part = lax.ppermute(part, "tp", swap)
    other_weights = (part, across(part, 1))

    source = jnp.concatenate([queries, keys, values], axis=0)
    _, tall = part_rows(rows, range(2, BRANCHES))
    first, second, own, core, chip = call(
        functools.partial(split_kernel, sets, scale, dim),
        [shape(each * tall, LANES)] * 2 + [shape(part * rows, LANES) for part in (3, 6, 3)],
        2,
        (head_offset, index, source),
        1.0,
        vmem=12,
    )
    wide = [across(first, 2), across(second, 3)]
    core = across(core, 1)
    own_chip, first, second, relay, selects, spreads, own_picked, own_tight = call(
        functools.partial(own_chip_kernel, sets, rows, dim),
        [shape(each, 2, rows, LANES, dtype=jnp.float32)] + [shape(each * tall, LANES)] * 2
        + [shape(6 * rows, LANES)]
        + [shape(each, rows, rows)] * 2
        + [shape(2, rows, LANES), shape(each, 2, rows // 2, LANES)],
        2,
        (head_offset, index, own, core, chip),
        2.4,
        [pltpu.VMEM((2, rows, LANES), bf16), pltpu.VMEM((each, 2, rows, LANES), bf16)],
        vmem=12,
    )
    at, all_rows = set_rows(sets, rows, each)
    *turned, relay = call(
        functools.partial(turn_kernel, at),
        [shape(NEAR, all_rows - first, LANES) for first in at] + [shape(6 * rows, LANES)],
        1,
        (index, first, second, *wide, relay),
        0.3,
        passed=True,
    )
    chip = across(relay, 2)
    far = [
        across(turned[first_set(sets, step)], NEAR * step)
        for step in range(max(span for span, _ in sets))
    ]

    near, tight_done, tight_top, picked_queries, residual = call(
        functools.partial(local_kernel, rows, dim),
        [
            shape(each, NEAR, rows, LANES, dtype=jnp.float32),
            shape(each, NEAR, rows // 2, LANES, dtype=jnp.float32),
            shape(each, rows // 2, LANES, dtype=jnp.float32),
            shape(NEAR, rows // 2, LANES),
            shape(rows, cols),
        ],
        1,
        (index, chip, own_chip, selects, own_picked, own_tight, residual_in),
        3.4,
        [
            pltpu.VMEM((2, rows, LANES), bf16),
            pltpu.VMEM((each, 2, rows, LANES), bf16),
            pltpu.VMEM((each, NEAR, rows // 2, LANES), bf16),
            pltpu.VMEM((NEAR, rows // 2, LANES), bf16),
        ],
        vmem=12,
    )
    mixes = call(
        functools.partial(finish_kernel, sets, rows, dim),
        [shape(rows, LANES)] * NEAR,
        2,
        (head_offset, index, *far, picked_queries, near, tight_done, tight_top, selects, spreads),
        6.0,
        [
            pltpu.VMEM((each, NEAR, rows, LANES), jnp.float32),
            pltpu.VMEM((each, rows, LANES), jnp.float32),
            pltpu.VMEM((NEAR, rows, LANES), bf16),
        ],
        vmem=16,
    )
    mixes = [mixes[0], across(mixes[1], 1), across(mixes[2], 2), mixes[3]]
    held, both = call(
        hold_kernel,
        [shape(rows, LANES), shape(2 * rows, LANES)],
        0,
        (mixes[3], mixes[0], mixes[1]),
        0.2,
    )
    mixes[3] = across(held, 3)
    step = rows // CHUNKS
    parts = call(halve_kernel, [shape(2 * step, LANES)] * CHUNKS, 0, mixes[2:], 0.2)
    both = lax.ppermute(both, "tp", swap)
    parts = [lax.ppermute(block, "tp", swap) for block in parts]
    other_residual = lax.ppermute(residual, "tp", swap)
    width = norm_gain.shape[0]
    mine, theirs = [], []
    own = call(
        own_kernel,
        shape(rows, width, dtype=jnp.float32),
        1,
        (index, residual_in, other_residual, out_weight, *mixes),
        1.2,
        [pltpu.VMEM((rows, cols), bf16)],
    )
    for number in range(CHUNKS):
        part = slice(number * step, (number + 1) * step)
        places = [(0, part.start), (0, rows + part.start), (1, 0), (1, step)]
        send, keep = call(
            functools.partial(block_kernel, part, places),
            [shape(step, cols), shape(step, cols, dtype=jnp.float32)],
            1,
            (
                index,
                own,
                both,
                parts[number],
                *other_weights,
                norm_gain.reshape(1, width),
                gate_weight,
                up_weight,
                down_weight,
            ),
            2.0,
            [
                pltpu.VMEM((step, width), jnp.float32),
                pltpu.VMEM((step, gate_weight.shape[1]), bf16),
                pltpu.VMEM((step, cols), bf16),
            ],
        )
        mine.append(keep)
        theirs.append(lax.ppermute(send, "tp", swap))
    return call(add_kernel, shape(rows, cols), 0, (*mine, *theirs), 0.8)


def solution(mesh):
    placed = (
        P("seq", "tp"),
        P("seq", "tp"),
        P("seq", "tp"),
        P("seq", "tp"),
        P(None, "tp"),
        P("tp", None),
        P(),
        P(None, "tp"),
        P(None, "tp"),
        P("tp", None),
    )
    return jax.shard_map(
        shards, mesh=mesh, in_specs=placed, out_specs=P("seq", "tp"), check_vma=False
    )
```

```python
import functools
import math

import jax
import jax.numpy as jnp
from jax import lax
from jax.experimental import pallas as pl
from jax.experimental.pallas import tpu as pltpu
from jax.sharding import PartitionSpec as P

BRANCHES = 6
LANES = 128
NEAR = 4
GROUP = LANES // NEAR
PEAK_FLOPS = 1153.5e12
MIB = 1024 * 1024
CHUNKS = 2
BLOCK = 256

masked_score = -1e30


def part_rows(rows, branches):
    first, at = 0, {}
    for branch in branches:
        at[branch] = first
        first += rows // 2**branch
    return at, first


def far_sets(seq_count, rows):
    top_bits = min(seq_count.bit_length() - 1, BRANCHES)
    sets = {}
    for branch in range(2, BRANCHES):
        sets.setdefault(2 ** min(branch + 1, top_bits) // NEAR, []).append(branch)
    return sorted(sets.items())


def set_rows(sets, rows, each):
    first, at = 0, []
    for _, branches in sets:
        at.append(first)
        first += each * sum(rows // 2**branch for branch in branches)
    return at, first


def first_set(sets, step):
    return min(number for number, (span, _) in enumerate(sets) if span > step)


def even(count):
    return -(-count // 16) * 16


def mask_select(rows, branch, offset):
    rate = 2**branch
    count = rows // rate
    row = lax.broadcasted_iota(jnp.int32, (count, rows), 0)
    col = lax.broadcasted_iota(jnp.int32, (count, rows), 1)
    return jnp.where(col == row * rate + (offset & (rate - 1)), 1.0, 0.0)


def selection(rows, branches, offset_ref, head):
    select = [mask_select(rows, branch, offset_ref[branch, head]) for branch in branches]
    return jnp.concatenate(select, axis=0).astype(jnp.bfloat16)


def far_picks(sets, rows, dim, blocks, selects):
    each = LANES // dim
    far_branches = range(2, BRANCHES)
    starts, _ = part_rows(rows, far_branches)
    picked = []
    for (key, value), mine in zip(blocks, selects):
        for head in range(each):
            lanes = slice(head * dim, (head + 1) * dim)
            pairs = jnp.concatenate([key[:, lanes], value[:, lanes]], axis=1)
            picked.append(jnp.dot(mine[head], pairs, preferred_element_type=jnp.float32))
    outs = []
    for number in range(len(blocks)):
        parts = []
        for _, branches in sets:
            for branch in branches:
                first, last = starts[branch], starts[branch] + rows // 2**branch
                parts += [picked[number * each + head][first:last] for head in range(each)]
        outs.append(jnp.concatenate(parts, axis=0).astype(jnp.bfloat16))
    return outs


def split_kernel(sets, scale, dim, offset_ref, index_ref, source_ref, *out_refs):
    wide_refs, own_ref, core_ref, chip_ref = out_refs[:2], *out_refs[2:]
    rows = source_ref.shape[0] // 3
    low = index_ref[0] % NEAR
    all_lanes = [
        pl.ds(pl.multiple_of((low ^ side) * LANES, LANES), LANES) for side in range(NEAR)
    ]
    blocks = [
        (source_ref[rows : 2 * rows, lanes], source_ref[2 * rows :, lanes]) for lanes in all_lanes[2:]
    ]
    each = LANES // dim
    selects = [
        [selection(rows, range(2, BRANCHES), offset_ref, (low ^ side) * each + head) for head in range(each)]
        for side in (2, 3)
    ]
    picks = far_picks(sets, rows, dim, blocks, selects)
    for pick, wide_ref in zip(picks, wide_refs):
        wide_ref[...] = pick
    for side, lanes in enumerate(all_lanes):
        ref, first = ((own_ref, 0), (core_ref, 0), (chip_ref, 0), (core_ref, 3 * rows))[side]
        ref[first : first + rows] = source_ref[:rows, lanes] * jnp.asarray(scale, jnp.bfloat16)
        ref[first + rows : first + 3 * rows] = source_ref[rows:, lanes]


def turn_kernel(at, index_ref, *refs):
    in_refs, out_refs = refs[:NEAR], refs[NEAR + 1 : -1]
    low = index_ref[0] % NEAR
    for side in range(NEAR):
        for first, out_ref in zip(at, out_refs):
            out_ref[low ^ side] = in_refs[side][first:, :]


def attend(jobs, batch):
    dim = jobs[0][0].shape[1]
    lane = lax.broadcasted_iota(jnp.int32, (1, LANES), 1)
    keys = [pairs[:, :dim] for _, pairs, _, _ in jobs]
    values = [jnp.where(lane < dim, jnp.ones_like(pairs), pairs) for _, pairs, _, _ in jobs]
    pieces = []
    for number, (query, _, _, _) in enumerate(jobs):
        block = min(BLOCK, query.shape[0])
        pieces += [(start, number, block) for start in range(0, query.shape[0], block)]
    pieces.sort(key=lambda piece: piece[0])
    done = {}
    for at in range(0, len(pieces), batch):
        now = pieces[at : at + batch]
        scores = []
        for start, number, block in now:
            query, _, before, _ = jobs[number]
            scores.append(
                lax.dot_general(
                    query[start : start + block],
                    keys[number][: before + start + block],
                    (((1,), (1,)), ((), ())),
                    preferred_element_type=jnp.float32,
                )
            )
        masked = []
        for (start, number, block), score in zip(now, scores):
            _, _, before, columns = jobs[number]
            end = before + start + block
            if before == 0 and block % LANES == 0:
                row = lax.broadcasted_iota(jnp.int32, (block, block), 0)
                col = lax.broadcasted_iota(jnp.int32, (block, block), 1)
                last = jnp.where(col <= row, score[:, start:], masked_score)
                masked.append(jnp.concatenate([score[:, :start], last], axis=1) if start else last)
            else:
                row = lax.broadcasted_iota(jnp.int32, (block, end), 0)
                allowed = columns[:, :end] <= row + (before + start)
                masked.append(jnp.where(allowed, score, masked_score))
        tops = [jnp.max(score, axis=1, keepdims=True) for score in masked]
        weights = [jnp.exp(score - top).astype(jnp.bfloat16) for score, top in zip(masked, tops)]
        for piece, weight, top in zip(now, weights, tops):
            start, number, block = piece
            end = jobs[number][2] + start + block
            accum = jnp.dot(weight, values[number][:end], preferred_element_type=jnp.float32)
            done.setdefault(number, []).append((top, accum))
    return [
        tuple(jnp.concatenate(column, axis=0) for column in zip(*done[number]))
        for number in range(len(jobs))
    ]


def top_lanes(top, count, branch):
    length = top.shape[0]
    high = top.astype(jnp.bfloat16).astype(jnp.float32)
    middle = (top - high).astype(jnp.bfloat16).astype(jnp.float32)
    low = top - high - middle
    lane = lax.broadcasted_iota(jnp.int32, (length, LANES), 1)
    row = lax.broadcasted_iota(jnp.int32, (length, LANES), 0)
    lane = lane - ((row >> (count.bit_length() - 1)) * GROUP + 3 * branch)
    parts = jnp.where(lane == 0, high, jnp.where(lane == 1, middle, jnp.where(lane == 2, low, 0.0)))
    return jnp.sum(parts.reshape(NEAR, count, LANES), axis=0)


def nearest(members, rows, dim, low, query, pairs):
    each = LANES // dim
    for side, (query_in, key_in, value_in) in members:
        core = (low ^ side) % 2
        query[core] = query_in
        for head in range(each):
            lanes = slice(head * dim, (head + 1) * dim)
            pairs[head, core] = jnp.concatenate([key_in[:, lanes], value_in[:, lanes]], axis=1)
    return [
        (
            query[:, :, head * dim : (head + 1) * dim].reshape(2 * rows, dim),
            pairs[head].reshape(2 * rows, LANES),
            0,
            None,
        )
        for head in range(each)
    ]


def nearest_out(top, accum):
    lane = lax.broadcasted_iota(jnp.int32, (1, LANES), 1)
    return jnp.where(lane == 0, top, accum).reshape(2, top.shape[0] // 2, LANES)


def raw_blocks(ref, rows, first=0):
    return tuple(ref[first + part * rows : first + (part + 1) * rows] for part in range(3))


def local_picks(rows, dim, block, select_ref):
    query, key, value = block
    each = LANES // dim
    left = lax.broadcasted_iota(jnp.int32, (1, LANES), 1) < dim
    both = [jnp.dot(select_ref[head], query, preferred_element_type=jnp.float32) for head in range(each)]
    pairs = []
    for head in range(each):
        lanes = slice(head * dim, (head + 1) * dim)
        pair = jnp.concatenate([key[:, lanes], value[:, lanes]], axis=1)
        pair = jnp.dot(select_ref[head, : rows // 2], pair, preferred_element_type=jnp.float32)
        pairs.append(pair.astype(jnp.bfloat16))
    return jnp.where(left, both[0], both[1]).astype(jnp.bfloat16), pairs


def own_chip_kernel(sets, rows, dim, offset_ref, index_ref, own_ref, pair_ref, chip_ref, *refs):
    near_ref, pick_refs, relay_ref = refs[0], refs[1:3], refs[3]
    select_ref, spread_ref, picked_ref, tight_ref, query, pairs = refs[4:]
    half = chip_ref.shape[0]
    relay_ref[:half] = chip_ref[...]
    relay_ref[half:] = pair_ref[half:]
    each = LANES // dim
    low = index_ref[0] % NEAR
    starts, used = part_rows(rows, range(1, BRANCHES))
    column = lax.broadcasted_iota(jnp.int32, (1, rows), 1)
    row_wide = lax.broadcasted_iota(jnp.int32, (rows, rows), 0)
    for head in range(each):
        select = [mask_select(rows, b, offset_ref[b, low * each + head]) for b in range(1, BRANCHES)]
        select.append(jnp.zeros((rows - used, rows), jnp.float32))
        select_ref[head] = jnp.concatenate(select, axis=0).astype(jnp.bfloat16)
        target = jnp.full((1, rows), -1, jnp.int32)
        for branch in range(1, BRANCHES):
            rate = 2**branch
            offset = offset_ref[branch, low * each + head] & (rate - 1)
            target = jnp.where(
                column >= starts[branch], (column - starts[branch]) * rate + offset, target
            )
        spread_ref[head] = jnp.where(row_wide == target, 1.0, 0.0).astype(jnp.bfloat16)
    members = [(side, raw_blocks(ref, rows)) for side, ref in enumerate((own_ref, pair_ref))]
    selects = [select_ref[head, rows // 2 : used] for head in range(each)]
    blocks = [block[1:] for _, block in members]
    for pick, pick_ref in zip(far_picks(sets, rows, dim, blocks, [selects, selects]), pick_refs):
        pick_ref[...] = pick
    for side, block in members:
        picked, tight = local_picks(rows, dim, block, select_ref)
        core = (low ^ side) % 2
        picked_ref[core] = picked
        for head in range(each):
            tight_ref[head, core] = tight[head]
    jobs = nearest(members, rows, dim, low, query, pairs)
    for head, (top, accum) in enumerate(attend(jobs, 4)):
        near_ref[head] = nearest_out(top, accum)


def local_kernel(rows, dim, index_ref, *refs):
    chip_ref, own_chip_ref, select_ref, own_picked_ref, own_tight_ref, residual_ref = refs[:6]
    near_ref, far_ref, top_ref, picked_ref, residual_out = refs[6:11]
    query, pairs, tight_pairs, tight_query = refs[11:]
    residual_out[...] = residual_ref[...]
    each = LANES // dim
    low = index_ref[0] % NEAR
    chip = low // 2
    count = rows // 2
    blocks = {side: raw_blocks(chip_ref, rows, 3 * rows * (side - 2)) for side in (2, 3)}
    for core in range(2):
        tight_query[chip * 2 + core] = own_picked_ref[core, :count]
        picked_ref[chip * 2 + core] = own_picked_ref[core, count:]
        for head in range(each):
            tight_pairs[head, chip * 2 + core] = own_tight_ref[head, core]
    for side in (2, 3):
        picked, tight = local_picks(rows, dim, blocks[side], select_ref)
        tight_query[low ^ side] = picked[:count]
        picked_ref[low ^ side] = picked[count:]
        for head in range(each):
            tight_pairs[head, low ^ side] = tight[head]
    members = [(side, blocks[side]) for side in range(2, NEAR)]
    jobs = nearest(members, rows, dim, low, query, pairs)
    for head in range(each):
        near_ref[head, pl.ds(chip * 2, 2)] = own_chip_ref[head]
        jobs.append(
            (
                tight_query[:, :, head * dim : (head + 1) * dim].reshape(NEAR * count, dim),
                tight_pairs[head].reshape(NEAR * count, LANES),
                0,
                None,
            )
        )
    results = attend(jobs, 4)
    for head in range(each):
        near_ref[head, pl.ds((chip ^ 1) * 2, 2)] = nearest_out(*results[head])
        top, accum = results[each + head]
        far_ref[head] = accum.reshape(NEAR, count, LANES)
        top_ref[head] = top_lanes(top, count, 1)


def far_work(sets, rows, dim, index_ref, far_refs, query_ref, far, tops):
    each = LANES // dim
    group = index_ref[0] // NEAR
    starts, _ = part_rows(rows, range(1, BRANCHES))
    query_at, _ = part_rows(rows, range(2, BRANCHES))
    at, _ = set_rows(sets, rows, each)
    jobs, slots = [], []
    for number, (span, branches) in enumerate(sets):
        place = group % span
        first = at[number]
        for branch in branches:
            count = rows // 2**branch
            length = NEAR * count
            col = lax.broadcasted_iota(jnp.int32, (1, span * length), 1)
            step = span - 1 - (col >> (length.bit_length() - 1))
            columns = jnp.where((step == 0) | ((place ^ step) < place), col, 1 << 30)
            queries = query_ref[:, query_at[branch] : query_at[branch] + even(count), :]
            blocks = []
            for far_step in reversed(range(span)):
                skip = first - at[first_set(sets, far_step)]
                blocks.append(far_refs[far_step][:, skip : skip + each * count, :])
            if count % 16:
                queries = queries.astype(jnp.float32)[:, :count]
                blocks = [block.astype(jnp.float32) for block in blocks]
            for head in range(each):
                pairs = [block[:, head * count : (head + 1) * count].reshape(length, LANES) for block in blocks]
                pairs = jnp.concatenate(pairs, axis=0).astype(jnp.bfloat16)
                query = queries[:, :, head * dim : (head + 1) * dim].reshape(length, dim)
                jobs.append((query.astype(jnp.bfloat16), pairs, (span - 1) * length, columns))
                slots.append((branch, head, count))
            first += each * count
    for (branch, head, count), (top, accum) in zip(slots, attend(jobs, 2 * len(jobs))):
        into = slice(starts[branch], starts[branch] + count)
        far[head, :, into, :] = accum.reshape(NEAR, count, LANES)
        tops[head, into, :] = top_lanes(top, count, branch)


def hold_kernel(block_ref, own_ref, core_ref, out_ref, both_ref):
    out_ref[...] = block_ref[...]
    rows = own_ref.shape[0]
    both_ref[:rows] = own_ref[...]
    both_ref[rows:] = core_ref[...]


def finish_kernel(sets, rows, dim, offset_ref, index_ref, *refs):
    steps = max(span for span, _ in sets)
    far_refs, refs = refs[:steps], refs[steps:]
    query_ref, near_ref, tight_ref, tight_top_ref, select_ref, spread_ref, refs = *refs[:6], refs[6:]
    out_refs, far, tops, mixed_ref = refs[:NEAR], *refs[NEAR:]
    each = LANES // dim
    low = index_ref[0] % NEAR
    starts, used = part_rows(rows, range(1, BRANCHES))
    tight = rows // 2
    for head in range(each):
        far[head, :, :tight, :] = tight_ref[head]
        far[head, :, used:, :] = jnp.zeros((NEAR, rows - used, LANES), jnp.float32)
        tops[head, :tight, :] = tight_top_ref[head]
        tops[head, used:, :] = jnp.zeros((rows - used, LANES), jnp.float32)
    far_work(sets, rows, dim, index_ref, far_refs, query_ref, far, tops)

    lane = lax.broadcasted_iota(jnp.int32, (1, LANES), 1)
    inside = lane % GROUP
    row = lax.broadcasted_iota(jnp.int32, (rows, 1), 0)
    row_lane = lax.broadcasted_iota(jnp.int32, (rows, LANES), 0)

    def along(start_of, value_of, fill):
        result = jnp.full(start_of.shape, fill, jnp.int32)
        for branch in range(1, BRANCHES):
            result = jnp.where(start_of >= starts[branch], value_of(branch), result)
        return result

    masks = jnp.zeros((1, LANES), jnp.int32)
    for branch in range(1, BRANCHES):
        masks = jnp.where(inside == 3 * branch, 2**branch - 1, masks)
    own_lane = along(row, lambda branch: 3 * branch, 0)

    def turned(array, lanes):
        return pltpu.roll(array, lanes % LANES, 1)

    heads = range(each)
    covered = []
    for head in heads:
        offsets = {
            branch: offset_ref[branch, low * each + head] & (2**branch - 1)
            for branch in range(1, BRANCHES)
        }
        chosen = jnp.where(inside == 0, 0, 1)
        for branch in range(1, BRANCHES):
            chosen = jnp.where(inside == 3 * branch, offsets[branch], chosen)
        covered.append((row_lane & masks) == chosen)
    stats = [
        jnp.dot(spread_ref[head], tops[head].astype(jnp.bfloat16), preferred_element_type=jnp.float32)
        for head in heads
    ]
    stats = [block + turned(block, -1) + turned(block, -2) for block in stats]
    for member in range(NEAR):
        stats = [
            jnp.where(lane == GROUP * member, near_ref[head, member][:, 0:1], stats[head]) for head in heads
        ]
    stats = [jnp.where(covered[head], stats[head], masked_score) for head in heads]
    peaks = stats
    for step in (3, 6, 12):
        peaks = [jnp.maximum(peak, turned(peak, -step)) for peak in peaks]
    peaks = [jnp.where(inside == 0, peak, masked_score) for peak in peaks]
    for step in (3, 6, 12):
        peaks = [jnp.maximum(peak, turned(peak, step)) for peak in peaks]
    weight = [
        jnp.where(block > 0.5 * masked_score, jnp.exp(block - peak), 0.0)
        for block, peak in zip(stats, peaks)
    ]
    weight = [block.astype(jnp.bfloat16) for block in weight]
    weights = [
        jnp.dot(select_ref[head], weight[head], preferred_element_type=jnp.float32) for head in heads
    ]
    from_lane = lax.broadcasted_iota(jnp.int32, (LANES, NEAR * LANES), 0)
    to_member = lax.broadcasted_iota(jnp.int32, (LANES, NEAR * LANES), 1) >> (LANES.bit_length() - 1)
    group = GROUP.bit_length() - 1
    any_lane = jnp.where(from_lane >> group == to_member, 1.0, 0.0).astype(jnp.bfloat16)
    first_lane = jnp.where(from_lane == to_member << group, 1.0, 0.0).astype(jnp.bfloat16)
    weights = [jnp.where(inside == own_lane, block, 0.0).astype(jnp.bfloat16) for block in weights]
    weights = [jnp.dot(block, any_lane, preferred_element_type=jnp.float32) for block in weights]
    owns = [jnp.dot(block, first_lane, preferred_element_type=jnp.float32) for block in weight]
    scaled = [[] for _ in heads]
    for member in range(NEAR):
        for head in heads:
            block = far[head, member] * weights[head][:, member * LANES : (member + 1) * LANES]
            rest = block - block.astype(jnp.bfloat16).astype(jnp.float32)
            scaled[head].append(jnp.where(lane == 0, rest, block).astype(jnp.bfloat16))
    added = [
        jnp.dot(spread_ref[head], jnp.concatenate(scaled[head], axis=1), preferred_element_type=jnp.float32)
        for head in heads
    ]
    halves = [[] for _ in heads]
    for member in range(NEAR):
        for head in heads:
            block = added[head][:, member * LANES : (member + 1) * LANES]
            own = owns[head][:, member * LANES : (member + 1) * LANES]
            total = block + own * near_ref[head, member]
            below = total[:, 1:2] + block[:, 0:1]
            halves[head].append(total[:, dim:] * (1.0 / below))
    for member in range(NEAR):
        pair = [mixed[member] for mixed in halves]
        mixed_ref[member] = jnp.concatenate(pair, axis=1).astype(jnp.bfloat16)
    for side in range(NEAR):
        out_refs[side][...] = mixed_ref[low ^ side]


def lay_out(low, block_refs, part, mix_ref):
    for side, ref in enumerate(block_refs):
        lanes = pl.ds(pl.multiple_of((low ^ side) * LANES, LANES), LANES)
        mix_ref[:, lanes] = ref[part, :]


def halve_kernel(first_ref, second_ref, *out_refs):
    step = out_refs[0].shape[0] // 2
    for number, out_ref in enumerate(out_refs):
        part = slice(number * step, (number + 1) * step)
        out_ref[:step] = first_ref[part, :]
        out_ref[step:] = second_ref[part, :]


def own_kernel(index_ref, residual_ref, other_residual_ref, weight_ref, *refs):
    block_refs, out_ref, mix_ref = refs[:NEAR], refs[NEAR], refs[NEAR + 1]
    rows, half = residual_ref.shape
    mine = pl.ds(pl.multiple_of(index_ref[1] * half, LANES), half)
    theirs = pl.ds(pl.multiple_of((1 - index_ref[1]) * half, LANES), half)
    lay_out(index_ref[0] % NEAR, block_refs, slice(0, rows), mix_ref)
    out_ref[...] = jnp.dot(mix_ref[...], weight_ref[...], preferred_element_type=jnp.float32)
    out_ref[:, mine] += residual_ref[...].astype(jnp.float32)
    out_ref[:, theirs] += other_residual_ref[...].astype(jnp.float32)


def block_kernel(part, places, index_ref, own_ref, *refs):
    block_refs, refs = refs[:2], refs[2:]
    first_weight_ref, second_weight_ref, gain_ref, gate_ref, up_ref, down_ref = refs[:6]
    theirs_ref, mine_ref, hidden_ref, act_ref, mix_ref = refs[6:]
    half = theirs_ref.shape[1]
    mine = pl.ds(pl.multiple_of(index_ref[1] * half, LANES), half)
    theirs = pl.ds(pl.multiple_of((1 - index_ref[1]) * half, LANES), half)
    count = first_weight_ref.shape[0]
    core = index_ref[0] % 2
    rows = mix_ref.shape[0]
    for side, (place, first) in enumerate(places):
        lanes = pl.ds(pl.multiple_of((index_ref[0] % NEAR ^ side) * LANES, LANES), LANES)
        mix_ref[:, lanes] = block_refs[place][first : first + rows, :]
    hidden = own_ref[part, :]
    for place, weight_ref in ((core, first_weight_ref), (1 - core, second_weight_ref)):
        lanes = pl.ds(pl.multiple_of(place * count, LANES), count)
        hidden += jnp.dot(mix_ref[:, lanes], weight_ref[...], preferred_element_type=jnp.float32)
    hidden_ref[...] = hidden
    inverse = lax.rsqrt(jnp.mean(hidden * hidden, axis=1, keepdims=True) + 1e-05)
    normed = (hidden * inverse * gain_ref[...]).astype(jnp.bfloat16)
    step = 256
    for first in range(0, act_ref.shape[1], step):
        gate = jnp.dot(normed, gate_ref[:, first : first + step], preferred_element_type=jnp.float32)
        up = jnp.dot(normed, up_ref[:, first : first + step], preferred_element_type=jnp.float32)
        act_ref[:, first : first + step] = (gate / (1.0 + jnp.exp(-gate)) * up).astype(jnp.bfloat16)
    act = act_ref[...]
    theirs_ref[...] = jnp.dot(act, down_ref[:, theirs], preferred_element_type=jnp.float32).astype(
        jnp.bfloat16
    )
    mine_ref[...] = hidden_ref[:, mine] + jnp.dot(
        act, down_ref[:, mine], preferred_element_type=jnp.float32
    )


def add_kernel(*refs):
    count = (len(refs) - 1) // 2
    out_ref = refs[-1]
    for number in range(count):
        mine, theirs = refs[number], refs[count + number]
        step = mine.shape[0]
        out_ref[number * step : (number + 1) * step, :] = (
            mine[...] + theirs[...].astype(jnp.float32)
        ).astype(out_ref.dtype)


def call(kernel, out_shape, smem, operands, micros, scratch=(), vmem=8, passed=False):
    specs = [
        pl.BlockSpec(memory_space=pltpu.SMEM if number < smem else pltpu.VMEM)
        for number in range(len(operands))
    ]
    out_specs = jax.tree.map(lambda _: pl.BlockSpec(memory_space=pltpu.VMEM), out_shape)
    aliases = {}
    if passed:
        specs[-1] = out_specs[-1] = pl.BlockSpec(memory_space=pl.ANY)
        aliases = {len(specs) - 1: len(out_specs) - 1}
    return pl.pallas_call(
        kernel,
        out_shape=out_shape,
        in_specs=specs,
        out_specs=out_specs,
        input_output_aliases=aliases,
        scratch_shapes=list(scratch),
        compiler_params=pltpu.CompilerParams(vmem_limit_bytes=vmem * MIB),
        cost_estimate=pl.CostEstimate(
            flops=int(micros * PEAK_FLOPS / 1e6), bytes_accessed=0, transcendentals=0
        ),
    )(*operands)


def shards(
    residual_in,
    queries,
    keys,
    values,
    head_offset,
    out_weight,
    norm_gain,
    gate_weight,
    up_weight,
    down_weight,
):
    rows, cols = queries.shape
    heads = head_offset.shape[1]
    dim = cols // heads
    each = heads // NEAR
    seq_count = lax.axis_size("seq")
    scale = 1.0 / math.sqrt(dim)
    sets = far_sets(seq_count, rows)
    index = jnp.stack([lax.axis_index("seq"), lax.axis_index("tp")]).astype(jnp.int32)
    bf16 = jnp.bfloat16

    def shape(*sizes, dtype=bf16):
        return jax.ShapeDtypeStruct(sizes, dtype)

    def across(block, distance):
        if distance == 0:
            return block
        return lax.ppermute(block, "seq", [(i, i ^ distance) for i in range(seq_count)])

    swap = [(0, 1), (1, 0)]
    half = out_weight.shape[0] // 2
    part = lax.dynamic_slice_in_dim(out_weight, lax.axis_index("seq") % 2 * half, half)
    part = lax.ppermute(part, "tp", swap)
    other_weights = (part, across(part, 1))

    source = jnp.concatenate([queries, keys, values], axis=0)
    _, tall = part_rows(rows, range(2, BRANCHES))
    first, second, own, core, chip = call(
        functools.partial(split_kernel, sets, scale, dim),
        [shape(each * tall, LANES)] * 2 + [shape(part * rows, LANES) for part in (3, 6, 3)],
        2,
        (head_offset, index, source),
        1.0,
        vmem=12,
    )
    wide = [across(first, 2), across(second, 3)]
    core = across(core, 1)
    own_chip, first, second, relay, selects, spreads, own_picked, own_tight = call(
        functools.partial(own_chip_kernel, sets, rows, dim),
        [shape(each, 2, rows, LANES, dtype=jnp.float32)] + [shape(each * tall, LANES)] * 2
        + [shape(6 * rows, LANES)]
        + [shape(each, rows, rows)] * 2
        + [shape(2, rows, LANES), shape(each, 2, rows // 2, LANES)],
        2,
        (head_offset, index, own, core, chip),
        2.4,
        [pltpu.VMEM((2, rows, LANES), bf16), pltpu.VMEM((each, 2, rows, LANES), bf16)],
        vmem=12,
    )
    at, all_rows = set_rows(sets, rows, each)
    *turned, relay = call(
        functools.partial(turn_kernel, at),
        [shape(NEAR, all_rows - first, LANES) for first in at] + [shape(6 * rows, LANES)],
        1,
        (index, first, second, *wide, relay),
        0.3,
        passed=True,
    )
    chip = across(relay, 2)
    far = [
        across(turned[first_set(sets, step)], NEAR * step)
        for step in range(max(span for span, _ in sets))
    ]

    near, tight_done, tight_top, picked_queries, residual = call(
        functools.partial(local_kernel, rows, dim),
        [
            shape(each, NEAR, rows, LANES, dtype=jnp.float32),
            shape(each, NEAR, rows // 2, LANES, dtype=jnp.float32),
            shape(each, rows // 2, LANES, dtype=jnp.float32),
            shape(NEAR, rows // 2, LANES),
            shape(rows, cols),
        ],
        1,
        (index, chip, own_chip, selects, own_picked, own_tight, residual_in),
        3.4,
        [
            pltpu.VMEM((2, rows, LANES), bf16),
            pltpu.VMEM((each, 2, rows, LANES), bf16),
            pltpu.VMEM((each, NEAR, rows // 2, LANES), bf16),
            pltpu.VMEM((NEAR, rows // 2, LANES), bf16),
        ],
        vmem=12,
    )
    mixes = call(
        functools.partial(finish_kernel, sets, rows, dim),
        [shape(rows, LANES)] * NEAR,
        2,
        (head_offset, index, *far, picked_queries, near, tight_done, tight_top, selects, spreads),
        6.0,
        [
            pltpu.VMEM((each, NEAR, rows, LANES), jnp.float32),
            pltpu.VMEM((each, rows, LANES), jnp.float32),
            pltpu.VMEM((NEAR, rows, LANES), bf16),
        ],
        vmem=16,
    )
    mixes = [mixes[0], across(mixes[1], 1), across(mixes[2], 2), mixes[3]]
    held, both = call(
        hold_kernel,
        [shape(rows, LANES), shape(2 * rows, LANES)],
        0,
        (mixes[3], mixes[0], mixes[1]),
        0.2,
    )
    mixes[3] = across(held, 3)
    step = rows // CHUNKS
    parts = call(halve_kernel, [shape(2 * step, LANES)] * CHUNKS, 0, mixes[2:], 0.2)
    both = lax.ppermute(both, "tp", swap)
    parts = [lax.ppermute(block, "tp", swap) for block in parts]
    other_residual = lax.ppermute(residual, "tp", swap)
    width = norm_gain.shape[0]
    mine, theirs = [], []
    own = call(
        own_kernel,
        shape(rows, width, dtype=jnp.float32),
        1,
        (index, residual_in, other_residual, out_weight, *mixes),
        1.2,
        [pltpu.VMEM((rows, cols), bf16)],
    )
    for number in range(CHUNKS):
        part = slice(number * step, (number + 1) * step)
        places = [(0, part.start), (0, rows + part.start), (1, 0), (1, step)]
        send, keep = call(
            functools.partial(block_kernel, part, places),
            [shape(step, cols), shape(step, cols, dtype=jnp.float32)],
            1,
            (
                index,
                own,
                both,
                parts[number],
                *other_weights,
                norm_gain.reshape(1, width),
                gate_weight,
                up_weight,
                down_weight,
            ),
            2.0,
            [
                pltpu.VMEM((step, width), jnp.float32),
                pltpu.VMEM((step, gate_weight.shape[1]), bf16),
                pltpu.VMEM((step, cols), bf16),
            ],
        )
        mine.append(keep)
        theirs.append(lax.ppermute(send, "tp", swap))
    return call(add_kernel, shape(rows, cols), 0, (*mine, *theirs), 0.8)


def solution(mesh):
    placed = (
        P("seq", "tp"),
        P("seq", "tp"),
        P("seq", "tp"),
        P("seq", "tp"),
        P(None, "tp"),
        P("tp", None),
        P(),
        P(None, "tp"),
        P(None, "tp"),
        P("tp", None),
    )
    return jax.shard_map(
        shards, mesh=mesh, in_specs=placed, out_specs=P("seq", "tp"), check_vma=False
    )
```

```python
import functools
import math

import jax
import jax.numpy as jnp
from jax import lax
from jax.experimental import pallas as pl
from jax.experimental.pallas import tpu as pltpu
from jax.sharding import PartitionSpec as P

BRANCHES = 6
LANES = 128
NEAR = 4
GROUP = LANES // NEAR
PEAK_FLOPS = 1153.5e12
MIB = 1024 * 1024
CHUNKS = 2

masked_score = -1e30


def part_rows(rows, branches):
    first, at = 0, {}
    for branch in branches:
        at[branch] = first
        first += rows // 2**branch
    return at, first


def far_sets(seq_count, rows):
    top_bits = min(seq_count.bit_length() - 1, BRANCHES)
    sets = {}
    for branch in range(2, BRANCHES):
        sets.setdefault(2 ** min(branch + 1, top_bits) // NEAR, []).append(branch)
    return sorted(sets.items())


def set_rows(sets, rows, each):
    first, at = 0, []
    for _, branches in sets:
        at.append(first)
        first += each * sum(rows // 2**branch for branch in branches)
    return at, first


def first_set(sets, step):
    return min(number for number, (span, _) in enumerate(sets) if span > step)


def even(count):
    return -(-count // 16) * 16


def mask_select(rows, branch, offset):
    rate = 2**branch
    count = rows // rate
    row = lax.broadcasted_iota(jnp.int32, (count, rows), 0)
    col = lax.broadcasted_iota(jnp.int32, (count, rows), 1)
    return jnp.where(col == row * rate + (offset & (rate - 1)), 1.0, 0.0)


def selection(rows, branches, offset_ref, head):
    select = [mask_select(rows, branch, offset_ref[branch, head]) for branch in branches]
    return jnp.concatenate(select, axis=0).astype(jnp.bfloat16)


def far_picks(sets, rows, dim, blocks, selects):
    each = LANES // dim
    far_branches = range(2, BRANCHES)
    starts, _ = part_rows(rows, far_branches)
    picked = []
    for (key, value), mine in zip(blocks, selects):
        for head in range(each):
            lanes = slice(head * dim, (head + 1) * dim)
            pairs = jnp.concatenate([key[:, lanes], value[:, lanes]], axis=1)
            picked.append(jnp.dot(mine[head], pairs, preferred_element_type=jnp.float32))
    outs = []
    for number in range(len(blocks)):
        parts = []
        for _, branches in sets:
            for branch in branches:
                first, last = starts[branch], starts[branch] + rows // 2**branch
                parts += [picked[number * each + head][first:last] for head in range(each)]
        outs.append(jnp.concatenate(parts, axis=0).astype(jnp.bfloat16))
    return outs


def split_kernel(sets, scale, dim, offset_ref, index_ref, source_ref, *out_refs):
    wide_refs, own_ref, core_ref, chip_ref = out_refs[:2], *out_refs[2:]
    rows = source_ref.shape[0] // 3
    low = index_ref[0] % NEAR
    all_lanes = [
        pl.ds(pl.multiple_of((low ^ side) * LANES, LANES), LANES) for side in range(NEAR)
    ]
    blocks = [
        (source_ref[rows : 2 * rows, lanes], source_ref[2 * rows :, lanes]) for lanes in all_lanes[2:]
    ]
    each = LANES // dim
    selects = [
        [selection(rows, range(2, BRANCHES), offset_ref, (low ^ side) * each + head) for head in range(each)]
        for side in (2, 3)
    ]
    picks = far_picks(sets, rows, dim, blocks, selects)
    for pick, wide_ref in zip(picks, wide_refs):
        wide_ref[...] = pick
    for side, lanes in enumerate(all_lanes):
        ref, first = ((own_ref, 0), (core_ref, 0), (chip_ref, 0), (core_ref, 3 * rows))[side]
        ref[first : first + rows] = source_ref[:rows, lanes] * jnp.asarray(scale, jnp.bfloat16)
        ref[first + rows : first + 3 * rows] = source_ref[rows:, lanes]


def turn_kernel(at, index_ref, *refs):
    in_refs, out_refs = refs[:NEAR], refs[NEAR + 1 : -1]
    low = index_ref[0] % NEAR
    for side in range(NEAR):
        for first, out_ref in zip(at, out_refs):
            out_ref[low ^ side] = in_refs[side][first:, :]


def attend(jobs, batch):
    dim = jobs[0][0].shape[1]
    lane = lax.broadcasted_iota(jnp.int32, (1, LANES), 1)
    keys = [pairs[:, :dim] for _, pairs, _, _ in jobs]
    values = [jnp.where(lane < dim, jnp.ones_like(pairs), pairs) for _, pairs, _, _ in jobs]
    pieces = []
    for number, (query, _, _, _) in enumerate(jobs):
        block = min(128, query.shape[0])
        pieces += [(start, number, block) for start in range(0, query.shape[0], block)]
    pieces.sort(key=lambda piece: piece[0])
    done = {}
    for at in range(0, len(pieces), batch):
        now = pieces[at : at + batch]
        scores = []
        for start, number, block in now:
            query, _, before, _ = jobs[number]
            scores.append(
                lax.dot_general(
                    query[start : start + block],
                    keys[number][: before + start + block],
                    (((1,), (1,)), ((), ())),
                    preferred_element_type=jnp.float32,
                )
            )
        masked = []
        for (start, number, block), score in zip(now, scores):
            _, _, before, columns = jobs[number]
            end = before + start + block
            if before == 0 and block == 128:
                row = lax.broadcasted_iota(jnp.int32, (block, block), 0)
                col = lax.broadcasted_iota(jnp.int32, (block, block), 1)
                last = jnp.where(col <= row, score[:, start:], masked_score)
                masked.append(jnp.concatenate([score[:, :start], last], axis=1) if start else last)
            else:
                row = lax.broadcasted_iota(jnp.int32, (block, end), 0)
                allowed = columns[:, :end] <= row + (before + start)
                masked.append(jnp.where(allowed, score, masked_score))
        tops = [jnp.max(score, axis=1, keepdims=True) for score in masked]
        weights = [jnp.exp(score - top).astype(jnp.bfloat16) for score, top in zip(masked, tops)]
        for piece, weight, top in zip(now, weights, tops):
            start, number, block = piece
            end = jobs[number][2] + start + block
            accum = jnp.dot(weight, values[number][:end], preferred_element_type=jnp.float32)
            done.setdefault(number, []).append((top, accum))
    return [
        tuple(jnp.concatenate(column, axis=0) for column in zip(*done[number]))
        for number in range(len(jobs))
    ]


def top_lanes(top, count, branch):
    length = top.shape[0]
    high = top.astype(jnp.bfloat16).astype(jnp.float32)
    middle = (top - high).astype(jnp.bfloat16).astype(jnp.float32)
    low = top - high - middle
    lane = lax.broadcasted_iota(jnp.int32, (length, LANES), 1)
    row = lax.broadcasted_iota(jnp.int32, (length, LANES), 0)
    lane = lane - ((row >> (count.bit_length() - 1)) * GROUP + 3 * branch)
    parts = jnp.where(lane == 0, high, jnp.where(lane == 1, middle, jnp.where(lane == 2, low, 0.0)))
    return jnp.sum(parts.reshape(NEAR, count, LANES), axis=0)


def nearest(members, rows, dim, low, query, pairs):
    each = LANES // dim
    for side, (query_in, key_in, value_in) in members:
        core = (low ^ side) % 2
        query[core] = query_in
        for head in range(each):
            lanes = slice(head * dim, (head + 1) * dim)
            pairs[head, core] = jnp.concatenate([key_in[:, lanes], value_in[:, lanes]], axis=1)
    return [
        (
            query[:, :, head * dim : (head + 1) * dim].reshape(2 * rows, dim),
            pairs[head].reshape(2 * rows, LANES),
            0,
            None,
        )
        for head in range(each)
    ]


def nearest_out(top, accum):
    lane = lax.broadcasted_iota(jnp.int32, (1, LANES), 1)
    return jnp.where(lane == 0, top, accum).reshape(2, top.shape[0] // 2, LANES)


def raw_blocks(ref, rows, first=0):
    return tuple(ref[first + part * rows : first + (part + 1) * rows] for part in range(3))


def local_picks(rows, dim, block, select_ref):
    query, key, value = block
    each = LANES // dim
    left = lax.broadcasted_iota(jnp.int32, (1, LANES), 1) < dim
    both = [jnp.dot(select_ref[head], query, preferred_element_type=jnp.float32) for head in range(each)]
    pairs = []
    for head in range(each):
        lanes = slice(head * dim, (head + 1) * dim)
        pair = jnp.concatenate([key[:, lanes], value[:, lanes]], axis=1)
        pair = jnp.dot(select_ref[head, : rows // 2], pair, preferred_element_type=jnp.float32)
        pairs.append(pair.astype(jnp.bfloat16))
    return jnp.where(left, both[0], both[1]).astype(jnp.bfloat16), pairs


def own_chip_kernel(sets, rows, dim, offset_ref, index_ref, own_ref, pair_ref, chip_ref, *refs):
    near_ref, pick_refs, relay_ref = refs[0], refs[1:3], refs[3]
    select_ref, spread_ref, picked_ref, tight_ref, query, pairs = refs[4:]
    half = chip_ref.shape[0]
    relay_ref[:half] = chip_ref[...]
    relay_ref[half:] = pair_ref[half:]
    each = LANES // dim
    low = index_ref[0] % NEAR
    starts, used = part_rows(rows, range(1, BRANCHES))
    column = lax.broadcasted_iota(jnp.int32, (1, rows), 1)
    row_wide = lax.broadcasted_iota(jnp.int32, (rows, rows), 0)
    for head in range(each):
        select = [mask_select(rows, b, offset_ref[b, low * each + head]) for b in range(1, BRANCHES)]
        select.append(jnp.zeros((rows - used, rows), jnp.float32))
        select_ref[head] = jnp.concatenate(select, axis=0).astype(jnp.bfloat16)
        target = jnp.full((1, rows), -1, jnp.int32)
        for branch in range(1, BRANCHES):
            rate = 2**branch
            offset = offset_ref[branch, low * each + head] & (rate - 1)
            target = jnp.where(
                column >= starts[branch], (column - starts[branch]) * rate + offset, target
            )
        spread_ref[head] = jnp.where(row_wide == target, 1.0, 0.0).astype(jnp.bfloat16)
    members = [(side, raw_blocks(ref, rows)) for side, ref in enumerate((own_ref, pair_ref))]
    selects = [select_ref[head, rows // 2 : used] for head in range(each)]
    blocks = [block[1:] for _, block in members]
    for pick, pick_ref in zip(far_picks(sets, rows, dim, blocks, [selects, selects]), pick_refs):
        pick_ref[...] = pick
    for side, block in members:
        picked, tight = local_picks(rows, dim, block, select_ref)
        core = (low ^ side) % 2
        picked_ref[core] = picked
        for head in range(each):
            tight_ref[head, core] = tight[head]
    jobs = nearest(members, rows, dim, low, query, pairs)
    for head, (top, accum) in enumerate(attend(jobs, 4)):
        near_ref[head] = nearest_out(top, accum)


def local_kernel(rows, dim, index_ref, *refs):
    chip_ref, own_chip_ref, select_ref, own_picked_ref, own_tight_ref, residual_ref = refs[:6]
    near_ref, far_ref, top_ref, picked_ref, residual_out = refs[6:11]
    query, pairs, tight_pairs, tight_query = refs[11:]
    residual_out[...] = residual_ref[...]
    each = LANES // dim
    low = index_ref[0] % NEAR
    chip = low // 2
    count = rows // 2
    blocks = {side: raw_blocks(chip_ref, rows, 3 * rows * (side - 2)) for side in (2, 3)}
    for core in range(2):
        tight_query[chip * 2 + core] = own_picked_ref[core, :count]
        picked_ref[chip * 2 + core] = own_picked_ref[core, count:]
        for head in range(each):
            tight_pairs[head, chip * 2 + core] = own_tight_ref[head, core]
    for side in (2, 3):
        picked, tight = local_picks(rows, dim, blocks[side], select_ref)
        tight_query[low ^ side] = picked[:count]
        picked_ref[low ^ side] = picked[count:]
        for head in range(each):
            tight_pairs[head, low ^ side] = tight[head]
    members = [(side, blocks[side]) for side in range(2, NEAR)]
    jobs = nearest(members, rows, dim, low, query, pairs)
    for head in range(each):
        near_ref[head, pl.ds(chip * 2, 2)] = own_chip_ref[head]
        jobs.append(
            (
                tight_query[:, :, head * dim : (head + 1) * dim].reshape(NEAR * count, dim),
                tight_pairs[head].reshape(NEAR * count, LANES),
                0,
                None,
            )
        )
    results = attend(jobs, 4)
    for head in range(each):
        near_ref[head, pl.ds((chip ^ 1) * 2, 2)] = nearest_out(*results[head])
        top, accum = results[each + head]
        far_ref[head] = accum.reshape(NEAR, count, LANES)
        top_ref[head] = top_lanes(top, count, 1)


def far_work(sets, rows, dim, index_ref, far_refs, query_ref, far, tops):
    each = LANES // dim
    group = index_ref[0] // NEAR
    starts, _ = part_rows(rows, range(1, BRANCHES))
    query_at, _ = part_rows(rows, range(2, BRANCHES))
    at, _ = set_rows(sets, rows, each)
    jobs, slots = [], []
    for number, (span, branches) in enumerate(sets):
        place = group % span
        first = at[number]
        for branch in branches:
            count = rows // 2**branch
            length = NEAR * count
            col = lax.broadcasted_iota(jnp.int32, (1, span * length), 1)
            step = span - 1 - (col >> (length.bit_length() - 1))
            columns = jnp.where((step == 0) | ((place ^ step) < place), col, 1 << 30)
            queries = query_ref[:, query_at[branch] : query_at[branch] + even(count), :]
            blocks = []
            for far_step in reversed(range(span)):
                skip = first - at[first_set(sets, far_step)]
                blocks.append(far_refs[far_step][:, skip : skip + each * count, :])
            if count % 16:
                queries = queries.astype(jnp.float32)[:, :count]
                blocks = [block.astype(jnp.float32) for block in blocks]
            for head in range(each):
                pairs = [block[:, head * count : (head + 1) * count].reshape(length, LANES) for block in blocks]
                pairs = jnp.concatenate(pairs, axis=0).astype(jnp.bfloat16)
                query = queries[:, :, head * dim : (head + 1) * dim].reshape(length, dim)
                jobs.append((query.astype(jnp.bfloat16), pairs, (span - 1) * length, columns))
                slots.append((branch, head, count))
            first += each * count
    for (branch, head, count), (top, accum) in zip(slots, attend(jobs, 5)):
        into = slice(starts[branch], starts[branch] + count)
        far[head, :, into, :] = accum.reshape(NEAR, count, LANES)
        tops[head, into, :] = top_lanes(top, count, branch)


def hold_kernel(block_ref, own_ref, core_ref, out_ref, both_ref):
    out_ref[...] = block_ref[...]
    rows = own_ref.shape[0]
    both_ref[:rows] = own_ref[...]
    both_ref[rows:] = core_ref[...]


def finish_kernel(sets, rows, dim, offset_ref, index_ref, *refs):
    steps = max(span for span, _ in sets)
    far_refs, refs = refs[:steps], refs[steps:]
    query_ref, near_ref, tight_ref, tight_top_ref, select_ref, spread_ref, refs = *refs[:6], refs[6:]
    out_refs, far, tops, mixed_ref = refs[:NEAR], *refs[NEAR:]
    each = LANES // dim
    low = index_ref[0] % NEAR
    starts, used = part_rows(rows, range(1, BRANCHES))
    tight = rows // 2
    for head in range(each):
        far[head, :, :tight, :] = tight_ref[head]
        far[head, :, used:, :] = jnp.zeros((NEAR, rows - used, LANES), jnp.float32)
        tops[head, :tight, :] = tight_top_ref[head]
        tops[head, used:, :] = jnp.zeros((rows - used, LANES), jnp.float32)
    far_work(sets, rows, dim, index_ref, far_refs, query_ref, far, tops)

    lane = lax.broadcasted_iota(jnp.int32, (1, LANES), 1)
    inside = lane % GROUP
    row = lax.broadcasted_iota(jnp.int32, (rows, 1), 0)
    row_lane = lax.broadcasted_iota(jnp.int32, (rows, LANES), 0)

    def along(start_of, value_of, fill):
        result = jnp.full(start_of.shape, fill, jnp.int32)
        for branch in range(1, BRANCHES):
            result = jnp.where(start_of >= starts[branch], value_of(branch), result)
        return result

    masks = jnp.zeros((1, LANES), jnp.int32)
    for branch in range(1, BRANCHES):
        masks = jnp.where(inside == 3 * branch, 2**branch - 1, masks)
    own_lane = along(row, lambda branch: 3 * branch, 0)

    def turned(array, lanes):
        return pltpu.roll(array, lanes % LANES, 1)

    heads = range(each)
    covered = []
    for head in heads:
        offsets = {
            branch: offset_ref[branch, low * each + head] & (2**branch - 1)
            for branch in range(1, BRANCHES)
        }
        chosen = jnp.where(inside == 0, 0, 1)
        for branch in range(1, BRANCHES):
            chosen = jnp.where(inside == 3 * branch, offsets[branch], chosen)
        covered.append((row_lane & masks) == chosen)
    stats = [
        jnp.dot(spread_ref[head], tops[head].astype(jnp.bfloat16), preferred_element_type=jnp.float32)
        for head in heads
    ]
    stats = [block + turned(block, -1) + turned(block, -2) for block in stats]
    for member in range(NEAR):
        stats = [
            jnp.where(lane == GROUP * member, near_ref[head, member][:, 0:1], stats[head]) for head in heads
        ]
    stats = [jnp.where(covered[head], stats[head], masked_score) for head in heads]
    peaks = stats
    for step in (3, 6, 12):
        peaks = [jnp.maximum(peak, turned(peak, -step)) for peak in peaks]
    peaks = [jnp.where(inside == 0, peak, masked_score) for peak in peaks]
    for step in (3, 6, 12):
        peaks = [jnp.maximum(peak, turned(peak, step)) for peak in peaks]
    weight = [
        jnp.where(block > 0.5 * masked_score, jnp.exp(block - peak), 0.0)
        for block, peak in zip(stats, peaks)
    ]
    weight = [block.astype(jnp.bfloat16) for block in weight]
    weights = [
        jnp.dot(select_ref[head], weight[head], preferred_element_type=jnp.float32) for head in heads
    ]
    from_lane = lax.broadcasted_iota(jnp.int32, (LANES, NEAR * LANES), 0)
    to_member = lax.broadcasted_iota(jnp.int32, (LANES, NEAR * LANES), 1) >> (LANES.bit_length() - 1)
    group = GROUP.bit_length() - 1
    any_lane = jnp.where(from_lane >> group == to_member, 1.0, 0.0).astype(jnp.bfloat16)
    first_lane = jnp.where(from_lane == to_member << group, 1.0, 0.0).astype(jnp.bfloat16)
    weights = [jnp.where(inside == own_lane, block, 0.0).astype(jnp.bfloat16) for block in weights]
    weights = [jnp.dot(block, any_lane, preferred_element_type=jnp.float32) for block in weights]
    owns = [jnp.dot(block, first_lane, preferred_element_type=jnp.float32) for block in weight]
    scaled = [[] for _ in heads]
    for member in range(NEAR):
        for head in heads:
            block = far[head, member] * weights[head][:, member * LANES : (member + 1) * LANES]
            rest = block - block.astype(jnp.bfloat16).astype(jnp.float32)
            scaled[head].append(jnp.where(lane == 0, rest, block).astype(jnp.bfloat16))
    added = [
        jnp.dot(spread_ref[head], jnp.concatenate(scaled[head], axis=1), preferred_element_type=jnp.float32)
        for head in heads
    ]
    halves = [[] for _ in heads]
    for member in range(NEAR):
        for head in heads:
            block = added[head][:, member * LANES : (member + 1) * LANES]
            own = owns[head][:, member * LANES : (member + 1) * LANES]
            total = block + own * near_ref[head, member]
            below = total[:, 1:2] + block[:, 0:1]
            halves[head].append(total[:, dim:] * (1.0 / below))
    for member in range(NEAR):
        pair = [mixed[member] for mixed in halves]
        mixed_ref[member] = jnp.concatenate(pair, axis=1).astype(jnp.bfloat16)
    for side in range(NEAR):
        out_refs[side][...] = mixed_ref[low ^ side]


def lay_out(low, block_refs, part, mix_ref):
    for side, ref in enumerate(block_refs):
        lanes = pl.ds(pl.multiple_of((low ^ side) * LANES, LANES), LANES)
        mix_ref[:, lanes] = ref[part, :]


def halve_kernel(first_ref, second_ref, *out_refs):
    step = out_refs[0].shape[0] // 2
    for number, out_ref in enumerate(out_refs):
        part = slice(number * step, (number + 1) * step)
        out_ref[:step] = first_ref[part, :]
        out_ref[step:] = second_ref[part, :]


def own_kernel(index_ref, residual_ref, other_residual_ref, weight_ref, *refs):
    block_refs, out_ref, mix_ref = refs[:NEAR], refs[NEAR], refs[NEAR + 1]
    rows, half = residual_ref.shape
    mine = pl.ds(pl.multiple_of(index_ref[1] * half, LANES), half)
    theirs = pl.ds(pl.multiple_of((1 - index_ref[1]) * half, LANES), half)
    lay_out(index_ref[0] % NEAR, block_refs, slice(0, rows), mix_ref)
    out_ref[...] = jnp.dot(mix_ref[...], weight_ref[...], preferred_element_type=jnp.float32)
    out_ref[:, mine] += residual_ref[...].astype(jnp.float32)
    out_ref[:, theirs] += other_residual_ref[...].astype(jnp.float32)


def block_kernel(part, places, index_ref, own_ref, *refs):
    block_refs, refs = refs[:2], refs[2:]
    first_weight_ref, second_weight_ref, gain_ref, gate_ref, up_ref, down_ref = refs[:6]
    theirs_ref, mine_ref, hidden_ref, act_ref, mix_ref = refs[6:]
    half = theirs_ref.shape[1]
    mine = pl.ds(pl.multiple_of(index_ref[1] * half, LANES), half)
    theirs = pl.ds(pl.multiple_of((1 - index_ref[1]) * half, LANES), half)
    count = first_weight_ref.shape[0]
    core = index_ref[0] % 2
    rows = mix_ref.shape[0]
    for side, (place, first) in enumerate(places):
        lanes = pl.ds(pl.multiple_of((index_ref[0] % NEAR ^ side) * LANES, LANES), LANES)
        mix_ref[:, lanes] = block_refs[place][first : first + rows, :]
    hidden = own_ref[part, :]
    for place, weight_ref in ((core, first_weight_ref), (1 - core, second_weight_ref)):
        lanes = pl.ds(pl.multiple_of(place * count, LANES), count)
        hidden += jnp.dot(mix_ref[:, lanes], weight_ref[...], preferred_element_type=jnp.float32)
    hidden_ref[...] = hidden
    inverse = lax.rsqrt(jnp.mean(hidden * hidden, axis=1, keepdims=True) + 1e-05)
    normed = (hidden * inverse * gain_ref[...]).astype(jnp.bfloat16)
    step = 256
    for first in range(0, act_ref.shape[1], step):
        gate = jnp.dot(normed, gate_ref[:, first : first + step], preferred_element_type=jnp.float32)
        up = jnp.dot(normed, up_ref[:, first : first + step], preferred_element_type=jnp.float32)
        act_ref[:, first : first + step] = (gate / (1.0 + jnp.exp(-gate)) * up).astype(jnp.bfloat16)
    act = act_ref[...]
    theirs_ref[...] = jnp.dot(act, down_ref[:, theirs], preferred_element_type=jnp.float32).astype(
        jnp.bfloat16
    )
    mine_ref[...] = hidden_ref[:, mine] + jnp.dot(
        act, down_ref[:, mine], preferred_element_type=jnp.float32
    )


def add_kernel(*refs):
    count = (len(refs) - 1) // 2
    out_ref = refs[-1]
    for number in range(count):
        mine, theirs = refs[number], refs[count + number]
        step = mine.shape[0]
        out_ref[number * step : (number + 1) * step, :] = (
            mine[...] + theirs[...].astype(jnp.float32)
        ).astype(out_ref.dtype)


def call(kernel, out_shape, smem, operands, micros, scratch=(), vmem=8, passed=False):
    specs = [
        pl.BlockSpec(memory_space=pltpu.SMEM if number < smem else pltpu.VMEM)
        for number in range(len(operands))
    ]
    out_specs = jax.tree.map(lambda _: pl.BlockSpec(memory_space=pltpu.VMEM), out_shape)
    aliases = {}
    if passed:
        specs[-1] = out_specs[-1] = pl.BlockSpec(memory_space=pl.ANY)
        aliases = {len(specs) - 1: len(out_specs) - 1}
    return pl.pallas_call(
        kernel,
        out_shape=out_shape,
        in_specs=specs,
        out_specs=out_specs,
        input_output_aliases=aliases,
        scratch_shapes=list(scratch),
        compiler_params=pltpu.CompilerParams(vmem_limit_bytes=vmem * MIB),
        cost_estimate=pl.CostEstimate(
            flops=int(micros * PEAK_FLOPS / 1e6), bytes_accessed=0, transcendentals=0
        ),
    )(*operands)


def shards(
    residual_in,
    queries,
    keys,
    values,
    head_offset,
    out_weight,
    norm_gain,
    gate_weight,
    up_weight,
    down_weight,
):
    rows, cols = queries.shape
    heads = head_offset.shape[1]
    dim = cols // heads
    each = heads // NEAR
    seq_count = lax.axis_size("seq")
    scale = 1.0 / math.sqrt(dim)
    sets = far_sets(seq_count, rows)
    index = jnp.stack([lax.axis_index("seq"), lax.axis_index("tp")]).astype(jnp.int32)
    bf16 = jnp.bfloat16

    def shape(*sizes, dtype=bf16):
        return jax.ShapeDtypeStruct(sizes, dtype)

    def across(block, distance):
        if distance == 0:
            return block
        return lax.ppermute(block, "seq", [(i, i ^ distance) for i in range(seq_count)])

    swap = [(0, 1), (1, 0)]
    half = out_weight.shape[0] // 2
    part = lax.dynamic_slice_in_dim(out_weight, lax.axis_index("seq") % 2 * half, half)
    part = lax.ppermute(part, "tp", swap)
    other_weights = (part, across(part, 1))

    source = jnp.concatenate([queries, keys, values], axis=0)
    _, tall = part_rows(rows, range(2, BRANCHES))
    first, second, own, core, chip = call(
        functools.partial(split_kernel, sets, scale, dim),
        [shape(each * tall, LANES)] * 2 + [shape(part * rows, LANES) for part in (3, 6, 3)],
        2,
        (head_offset, index, source),
        1.0,
        vmem=12,
    )
    wide = [across(first, 2), across(second, 3)]
    core = across(core, 1)
    own_chip, first, second, relay, selects, spreads, own_picked, own_tight = call(
        functools.partial(own_chip_kernel, sets, rows, dim),
        [shape(each, 2, rows, LANES, dtype=jnp.float32)] + [shape(each * tall, LANES)] * 2
        + [shape(6 * rows, LANES)]
        + [shape(each, rows, rows)] * 2
        + [shape(2, rows, LANES), shape(each, 2, rows // 2, LANES)],
        2,
        (head_offset, index, own, core, chip),
        2.4,
        [pltpu.VMEM((2, rows, LANES), bf16), pltpu.VMEM((each, 2, rows, LANES), bf16)],
        vmem=12,
    )
    at, all_rows = set_rows(sets, rows, each)
    *turned, relay = call(
        functools.partial(turn_kernel, at),
        [shape(NEAR, all_rows - first, LANES) for first in at] + [shape(6 * rows, LANES)],
        1,
        (index, first, second, *wide, relay),
        0.3,
        passed=True,
    )
    chip = across(relay, 2)
    far = [
        across(turned[first_set(sets, step)], NEAR * step)
        for step in range(max(span for span, _ in sets))
    ]

    near, tight_done, tight_top, picked_queries, residual = call(
        functools.partial(local_kernel, rows, dim),
        [
            shape(each, NEAR, rows, LANES, dtype=jnp.float32),
            shape(each, NEAR, rows // 2, LANES, dtype=jnp.float32),
            shape(each, rows // 2, LANES, dtype=jnp.float32),
            shape(NEAR, rows // 2, LANES),
            shape(rows, cols),
        ],
        1,
        (index, chip, own_chip, selects, own_picked, own_tight, residual_in),
        3.4,
        [
            pltpu.VMEM((2, rows, LANES), bf16),
            pltpu.VMEM((each, 2, rows, LANES), bf16),
            pltpu.VMEM((each, NEAR, rows // 2, LANES), bf16),
            pltpu.VMEM((NEAR, rows // 2, LANES), bf16),
        ],
        vmem=12,
    )
    mixes = call(
        functools.partial(finish_kernel, sets, rows, dim),
        [shape(rows, LANES)] * NEAR,
        2,
        (head_offset, index, *far, picked_queries, near, tight_done, tight_top, selects, spreads),
        6.0,
        [
            pltpu.VMEM((each, NEAR, rows, LANES), jnp.float32),
            pltpu.VMEM((each, rows, LANES), jnp.float32),
            pltpu.VMEM((NEAR, rows, LANES), bf16),
        ],
        vmem=16,
    )
    mixes = [mixes[0], across(mixes[1], 1), across(mixes[2], 2), mixes[3]]
    held, both = call(
        hold_kernel,
        [shape(rows, LANES), shape(2 * rows, LANES)],
        0,
        (mixes[3], mixes[0], mixes[1]),
        0.2,
    )
    mixes[3] = across(held, 3)
    step = rows // CHUNKS
    parts = call(halve_kernel, [shape(2 * step, LANES)] * CHUNKS, 0, mixes[2:], 0.2)
    both = lax.ppermute(both, "tp", swap)
    parts = [lax.ppermute(block, "tp", swap) for block in parts]
    other_residual = lax.ppermute(residual, "tp", swap)
    width = norm_gain.shape[0]
    mine, theirs = [], []
    own = call(
        own_kernel,
        shape(rows, width, dtype=jnp.float32),
        1,
        (index, residual_in, other_residual, out_weight, *mixes),
        1.2,
        [pltpu.VMEM((rows, cols), bf16)],
    )
    for number in range(CHUNKS):
        part = slice(number * step, (number + 1) * step)
        places = [(0, part.start), (0, rows + part.start), (1, 0), (1, step)]
        send, keep = call(
            functools.partial(block_kernel, part, places),
            [shape(step, cols), shape(step, cols, dtype=jnp.float32)],
            1,
            (
                index,
                own,
                both,
                parts[number],
                *other_weights,
                norm_gain.reshape(1, width),
                gate_weight,
                up_weight,
                down_weight,
            ),
            2.0,
            [
                pltpu.VMEM((step, width), jnp.float32),
                pltpu.VMEM((step, gate_weight.shape[1]), bf16),
                pltpu.VMEM((step, cols), bf16),
            ],
        )
        mine.append(keep)
        theirs.append(lax.ppermute(send, "tp", swap))
    return call(add_kernel, shape(rows, cols), 0, (*mine, *theirs), 0.8)


def solution(mesh):
    placed = (
        P("seq", "tp"),
        P("seq", "tp"),
        P("seq", "tp"),
        P("seq", "tp"),
        P(None, "tp"),
        P("tp", None),
        P(),
        P(None, "tp"),
        P(None, "tp"),
        P("tp", None),
    )
    return jax.shard_map(
        shards, mesh=mesh, in_specs=placed, out_specs=P("seq", "tp"), check_vma=False
    )
```
